256 devices in a mesh: space: 16 (over z_lo, x), filt: 16 (over y, z_hi, core).
Axes of the slice: x: 4, y: 4, z: 8 (z_hi: 2, z_lo: 4; z = z_hi * 4 + z_lo), core: 2. Of those that a mesh axis runs over, the one named last changes fastest.
Arguments:
- volume: bfloat16 [256, 16, 4096], P('filt', 'space'), may hold values from -6 to 6
- filters: bfloat16 [3, 3, 3, 256, 256], P(None, None, None, 'space', 'filt'), may hold values from -0.078125 to 0.078125
- cotangent: bfloat16 [256, 16, 4096], P('filt', 'space'), may hold values from -6 to 6
Outputs:
- output: bfloat16 [256, 16, 4096], P('filt', 'space')
- input_grad: bfloat16 [256, 16, 4096], P('filt', 'space')
The draws below stay inside these ranges and needn't reach their ends.
All inputs are finite; a program needn't handle non-finite values.
Results may differ from the reference program's by a relative error of at most 0.0013.
Values may be sent and summed in bfloat16 or wider, within the bound.
No kernel may reach another device: no remote copies, remote signals or barrier semaphores. Data moves between devices by JAX's collectives and lax.ppermute only.
A program may use at most 64 MiB of HBM per device.

```python
import jax
import jax.numpy as jnp
from jax import lax

C = 256
NY = 64
NZ = 64
NX = 16


def level_of(rng, dims, split, low, top_value):
    def one(axis_at, parts):
        draws = jax.random.uniform(jax.random.fold_in(jax.random.fold_in(rng, 6), axis_at), (parts,), jnp.float32, low / len(split), top_value / len(split))
        return jnp.repeat(jnp.exp(draws), dims[axis_at] // parts).reshape((-1,) + (1,) * (len(dims) - axis_at - 1))

    level = one(*split[0])
    for cut in split[1:]:
        level = level * one(*cut)
    return level


def noise(stream_key, shape, deviation, bound, pieces=(), kind=jnp.bfloat16):
    values = jax.random.normal(stream_key, shape, jnp.float32) * deviation
    if len(pieces) > 0:
        values = level_of(stream_key, shape, pieces, -0.22, 0.18) * values
    return jnp.clip(values, min=-bound, max=bound).astype(kind)


def setup_inputs(seed: int = 0) -> dict:
    arg_keys = jax.random.split(jax.random.key(seed), 4)
    volume = noise(arg_keys[0], (C, NX, NY * NZ), 1.0, 6.0, ((0, 16), (1, 16)))
    filters = noise(arg_keys[1], (3, 3, 3, C, C), (27 * C) ** -0.5, 0.078125, ((3, 16), (4, 16)))
    cotangent = noise(arg_keys[2], (C, NX, NY * NZ), 1.0, 6.0, ((0, 16), (1, 16)))
    return dict(volume=volume, filters=filters, cotangent=cotangent)


def convolve_full(volume_block, kernel):
    channels = volume_block.shape[0]
    planes = volume_block.shape[1]
    shaped = volume_block.reshape(channels, planes, NY, NZ).astype(jnp.float32)
    result = lax.conv_general_dilated(shaped[None], kernel.astype(jnp.float32), (1, 1, 1), [(1, 1), (1, 1), (1, 1)], dimension_numbers=("NCDHW", "DHWIO", "NCDHW"), preferred_element_type=jnp.float32)[0]
    return result.reshape(result.shape[0], planes, NY * NZ)


def reference(volume, filters, cotangent):
    output = convolve_full(volume, filters).astype(jnp.bfloat16)
    flipped = jnp.transpose(filters[::-1, ::-1, ::-1], (0, 1, 2, 4, 3))
    input_grad = convolve_full(cotangent, flipped).astype(jnp.bfloat16)
    return output, input_grad
```

```python
import functools

import jax
import jax.numpy as jnp
from jax import lax
from jax.experimental import pallas as pl
from jax.experimental.pallas import tpu as pltpu
from jax.sharding import Mesh
from jax.sharding import PartitionSpec as P

AXES = ("zl", "x", "y", "zh", "core")
SPACE = ("zl", "x")
FILT = ("y", "zh", "core")
BF16 = jnp.bfloat16
F32 = jnp.float32
VMEM = pl.BlockSpec(memory_space=pltpu.VMEM)
PARAMS = pltpu.CompilerParams(vmem_limit_bytes=48 * 1024 * 1024)

GROUPS = 8
CELLS = 512
CHUNKS = 5
ROWS = CHUNKS * 16
OFFSETS = 27


def call(kernel, out_shape, flops=0, byte_count=1 << 20, scratch=()):
    single = not isinstance(out_shape, (tuple, list))
    count = 1 if single else len(out_shape)
    return functools.partial(
        pl.pallas_call,
        kernel,
        out_shape=out_shape,
        out_specs=VMEM if single else [VMEM] * count,
        scratch_shapes=list(scratch),
        compiler_params=PARAMS,
        cost_estimate=pl.CostEstimate(flops=flops, bytes_accessed=byte_count, transcendentals=0),
    )


def run(kernel, out_shape, *args, **options):
    return call(kernel, out_shape, **options)(in_specs=[VMEM] * len(args))(*args)


def pack_kernel(volume_ref, cotangent_ref, filters_ref, out_ref):
    lane = lax.broadcasted_iota(jnp.int32, (16, 128), 1)
    for part, ref in enumerate((volume_ref, cotangent_ref)):
        whole = pltpu.roll(ref[...].astype(F32), 64, 1)
        edge = whole[:, :128]
        pieces = [jnp.where(lane < 64, 0.0, edge)]
        pieces += [whole[:, 128 * j : 128 * (j + 1)] for j in range(1, 32)]
        pieces += [jnp.where(lane < 64, edge, 0.0)]
        pieces = [piece.astype(BF16) for piece in pieces]
        for slab in range(GROUPS):
            for chunk in range(CHUNKS):
                row = part * ROWS + chunk * 16
                out_ref[slab, row : row + 16, :] = pieces[4 * slab + chunk]
    for low in range(4):
        pieces = []
        for high in range(8):
            d = high * 4 + low
            pieces.append(filters_ref[d] if d < OFFSETS else jnp.zeros((16, 16), BF16))
        block = jnp.concatenate(pieces, axis=1)
        for slab in range(GROUPS):
            out_ref[slab, 2 * ROWS + 16 * low : 2 * ROWS + 16 * (low + 1), :] = block


def unpack_kernel(packed_ref, acts_ref, weights_ref):
    acts_ref[...] = packed_ref[:, : 2 * ROWS, :]
    for d in range(OFFSETS):
        high, low = divmod(d, 4)
        row = 2 * ROWS + 16 * low
        weights_ref[d] = jnp.concatenate(
            [packed_ref[g, row : row + 16, 16 * high : 16 * (high + 1)] for g in range(GROUPS)],
            axis=1,
        )


def shifted(pieces):
    whole = jnp.concatenate(pieces, axis=0)
    middle = pltpu.roll(whole.astype(F32), 640 - 64, 1).astype(BF16)
    return whole[:, :CELLS], middle[:, :CELLS], whole[:, 128:]


def block_of(ref, group, first):
    return jnp.concatenate(
        [ref[group, first + 16 * c : first + 16 * (c + 1), :] for c in range(CHUNKS)], axis=1
    )


def weight(weights_ref, d):
    return jnp.concatenate([weights_ref[s % 4, s // 4, d] for s in range(16)], axis=0)


def combine(before, middle, after):
    place = lax.broadcasted_iota(jnp.int32, middle.shape, 1) % 64
    left = jnp.where(place > 0, pltpu.roll(before, 1, 1), 0.0)
    right = jnp.where(place < 63, pltpu.roll(after, CELLS - 1, 1), 0.0)
    return middle + left + right


def grad_kernel(low_ref, own_ref, high_ref, weights_ref, core_ref, keep_ref, send_ref, stack_ref, result_ref):
    for dx, ref in enumerate((high_ref, own_ref, low_ref)):
        above, same, below = shifted([block_of(ref, g, ROWS) for g in range(GROUPS)])
        for dy, value in enumerate((below, same, above)):
            row = (dx * 3 + dy) * 128
            stack_ref[row : row + 128, :] = value
    terms = []
    for dz in range(3):
        left = jnp.concatenate([weight(weights_ref, k * 3 + dz) for k in range(9)], axis=1)
        terms.append(jnp.dot(left, stack_ref[...], preferred_element_type=F32))
    result_ref[...] = combine(terms[2], terms[1], terms[0]).reshape(GROUPS, 2, 16, CELLS)
    core = core_ref[0]
    keep_ref[...] = result_ref[:, core]
    send_ref[...] = result_ref[:, 1 - core]


def forward_kernel(low_ref, own_ref, high_ref, other_ref, weights_ref, core_ref, out_ref, stack_ref):
    first = core_ref[0] == 0
    for dx, ref in enumerate((low_ref, own_ref, high_ref)):
        pieces = []
        for g in range(GROUPS):
            mine = block_of(ref, g, 0)
            theirs = block_of(other_ref.at[dx], g, 0)
            pieces.append(jnp.where(first, mine, theirs))
            pieces.append(jnp.where(first, theirs, mine))
        for dy, value in enumerate(shifted(pieces)):
            row = (dx * 3 + dy) * 256
            stack_ref[row : row + 256, :] = value
    terms = []
    for dz in range(3):
        left = jnp.concatenate([weight(weights_ref, k * 3 + dz) for k in range(9)], axis=0)
        terms.append(
            lax.dot_general(left, stack_ref[...], (((0,), (0,)), ((), ())), preferred_element_type=F32)
        )
    out_ref[...] = combine(*terms).astype(BF16).reshape(GROUPS, 16, CELLS)


def merge_kernel(output_ref, keep_ref, got_ref, out_ref):
    out_ref[:, :16, :] = output_ref[...]
    out_ref[:, 16:, :] = (keep_ref[...] + got_ref[...]).astype(BF16)


def split_kernel(packed_ref, output_ref, grad_ref):
    for g in range(GROUPS):
        output_ref[:, g * CELLS : (g + 1) * CELLS] = packed_ref[g, :16, :]
        grad_ref[:, g * CELLS : (g + 1) * CELLS] = packed_ref[g, 16:, :]


def local(volume, filters, cotangent):
    swap = [(0, 1), (1, 0)]
    core = lax.axis_index("core").astype(jnp.int32).reshape(1)
    packed = run(
        pack_kernel,
        jax.ShapeDtypeStruct((GROUPS, 2 * ROWS + 64, 128), BF16),
        volume.reshape(16, 4096),
        cotangent.reshape(16, 4096),
        filters.reshape(OFFSETS, 16, 16),
    )
    packed = lax.all_to_all(packed, ("y", "zh"), 0, 0)
    own, weights = run(
        unpack_kernel,
        [
            jax.ShapeDtypeStruct((GROUPS, 2 * ROWS, 128), BF16),
            jax.ShapeDtypeStruct((OFFSETS, 16, 128), BF16),
        ],
        packed,
    )
    up = [(i, i + 1) for i in range(15)]
    down = [(b, a) for a, b in up]
    low = lax.ppermute(own, SPACE, up)
    high = lax.ppermute(own, SPACE, down)
    weights = lax.all_to_all(jnp.broadcast_to(weights, (4,) + weights.shape), "zl", 0, 0)
    weights = lax.all_to_all(jnp.broadcast_to(weights, (4,) + weights.shape), "x", 0, 0)
    other = lax.ppermute(jnp.stack([low[:, :ROWS], own[:, :ROWS], high[:, :ROWS]]), "core", swap)
    flops = 2 * 27 * 256 * 128 * CELLS
    piece = jax.ShapeDtypeStruct((GROUPS, 16, CELLS), F32)
    smem = pl.BlockSpec(memory_space=pltpu.SMEM)
    keep, send = call(
        grad_kernel,
        [piece, piece],
        flops=flops,
        byte_count=4 << 20,
        scratch=[pltpu.VMEM((9 * 128, CELLS), BF16), pltpu.VMEM((GROUPS, 2, 16, CELLS), F32)],
    )(in_specs=[VMEM] * 4 + [smem])(low, own, high, weights, core)
    got = lax.ppermute(send, "core", swap)
    output = call(
        forward_kernel,
        jax.ShapeDtypeStruct((GROUPS, 16, CELLS), BF16),
        flops=flops,
        byte_count=4 << 20,
        scratch=[pltpu.VMEM((9 * 256, CELLS), BF16)],
    )(in_specs=[VMEM] * 5 + [smem])(low, own, high, other, weights, core)
    merged = run(merge_kernel, jax.ShapeDtypeStruct((GROUPS, 32, CELLS), BF16), output, keep, got)
    merged = lax.all_to_all(merged, ("y", "zh"), 0, 0)
    plane = jax.ShapeDtypeStruct((16, 4096), BF16)
    output, grad = run(split_kernel, [plane, plane], merged)
    return output.reshape(16, 1, 4096), grad.reshape(16, 1, 4096)


def solution(mesh):
    split = Mesh(mesh.devices.reshape(4, 4, 4, 2, 2), AXES)
    act = P(FILT, SPACE, None)
    return jax.shard_map(
        local,
        mesh=split,
        in_specs=(act, P(None, None, None, SPACE, FILT), act),
        out_specs=(act, act),
        check_vma=False,
    )
```

```python
import functools
import itertools

import jax
import jax.numpy as jnp
from jax import lax
from jax.experimental import pallas as pl
from jax.experimental.pallas import tpu as pltpu
from jax.sharding import Mesh
from jax.sharding import PartitionSpec as P

AXES = ("zl", "x", "y", "zh", "core")
SPACE = ("zl", "x")
FILT = ("y", "zh", "core")
BF16 = jnp.bfloat16
F32 = jnp.float32
VMEM = pl.BlockSpec(memory_space=pltpu.VMEM)
PARAMS = pltpu.CompilerParams(vmem_limit_bytes=48 * 1024 * 1024)

GROUPS = 8
CELLS = 512
CHUNKS = 5
ROWS = CHUNKS * 16
OFFSETS = 27
PART = 7


def index_of(zl, x, y, zh, core):
    return (((zl * 4 + x) * 4 + y) * 2 + zh) * 2 + core


def everyone():
    return itertools.product(range(4), range(4), range(4), range(2), range(2))


def first_groups():
    sides = itertools.product(range(4), range(4), range(2))
    groups = []
    for zl, other, zh in sides:
        groups.append([index_of(zl, k, other, zh, 0) for k in range(4)])
        groups.append([index_of(zl, other, k, zh, 1) for k in range(4)])
    return groups


def second_pairs(step):
    pairs = []
    for zl, x, y, zh, core in everyone():
        to = (zl, x, (y + step) % 4, zh, 0) if core == 0 else (zl, (x + step) % 4, y, zh, 1)
        pairs.append((index_of(zl, x, y, zh, core), index_of(*to)))
    return pairs


def call(kernel, out_shape, flops=0, byte_count=1 << 20, scratch=()):
    single = not isinstance(out_shape, (tuple, list))
    count = 1 if single else len(out_shape)
    return functools.partial(
        pl.pallas_call,
        kernel,
        out_shape=out_shape,
        out_specs=VMEM if single else [VMEM] * count,
        scratch_shapes=list(scratch),
        compiler_params=PARAMS,
        cost_estimate=pl.CostEstimate(flops=flops, bytes_accessed=byte_count, transcendentals=0),
    )


def run(kernel, out_shape, *args, **options):
    return call(kernel, out_shape, **options)(in_specs=[VMEM] * len(args))(*args)


def pack_kernel(volume_ref, cotangent_ref, filters_ref, out_ref):
    lane = lax.broadcasted_iota(jnp.int32, (16, 128), 1)
    for part, ref in enumerate((volume_ref, cotangent_ref)):
        whole = pltpu.roll(ref[...].astype(F32), 64, 1)
        edge = whole[:, :128]
        pieces = [jnp.where(lane < 64, 0.0, edge)]
        pieces += [whole[:, 128 * j : 128 * (j + 1)] for j in range(1, 32)]
        pieces += [jnp.where(lane < 64, edge, 0.0)]
        pieces = [piece.astype(BF16) for piece in pieces]
        for slab in range(GROUPS):
            for chunk in range(CHUNKS):
                row = part * ROWS + chunk * 16
                out_ref[slab, row : row + 16, :] = pieces[4 * slab + chunk]
    for quarter in range(4):
        pieces = []
        for d in range(quarter * PART, quarter * PART + 8):
            used = d < min(OFFSETS, (quarter + 1) * PART)
            pieces.append(filters_ref[d] if used else jnp.zeros((16, 16), BF16))
        block = jnp.concatenate(pieces, axis=1)
        for slab in (2 * quarter, 2 * quarter + 1):
            out_ref[slab, 2 * ROWS :, :] = block


def unpack_kernel(packed_ref, acts_ref, weights_ref):
    acts_ref[...] = packed_ref[:, : 2 * ROWS, :]
    for d in range(PART):
        piece = jnp.concatenate(
            [packed_ref[g, 2 * ROWS :, 16 * d : 16 * (d + 1)] for g in range(GROUPS)], axis=1
        )
        for copy in range(4):
            weights_ref[copy, d] = piece


def shifted(pieces):
    whole = jnp.concatenate(pieces, axis=0)
    middle = pltpu.roll(whole.astype(F32), 640 - 64, 1).astype(BF16)
    return whole[:, :CELLS], middle[:, :CELLS], whole[:, 128:]


def block_of(ref, group, first):
    return jnp.concatenate(
        [ref[group, first + 16 * c : first + 16 * (c + 1), :] for c in range(CHUNKS)], axis=1
    )


def weight(weights_ref, core, d):
    quarter, part = divmod(d, PART)
    rows = []
    for s in range(16):
        x = s % 4
        outer = jnp.where(core == 0, quarter, x)
        inner = jnp.where(core == 0, x, quarter)
        rows.append(weights_ref[outer, inner, s // 4, part])
    return jnp.concatenate(rows, axis=0)


def combine(before, middle, after):
    place = lax.broadcasted_iota(jnp.int32, middle.shape, 1) % 64
    left = jnp.where(place > 0, pltpu.roll(before, 1, 1), 0.0)
    right = jnp.where(place < 63, pltpu.roll(after, CELLS - 1, 1), 0.0)
    return middle + left + right


def grad_kernel(
    low_ref, own_ref, high_ref, mine_ref, next_ref, last_ref, far_a_ref, far_b_ref, place_ref,
    keep_ref, send_ref, weights_ref, stack_ref, result_ref,
):
    core, me = place_ref[0], place_ref[1]
    weights_ref[me] = mine_ref[...]
    weights_ref[lax.rem(me + 1, 4)] = next_ref[...]
    weights_ref[lax.rem(me + 3, 4)] = last_ref[...]
    weights_ref[lax.rem(me + 2, 4), :2] = far_a_ref[...]
    weights_ref[lax.rem(me + 2, 4), 2:] = far_b_ref[...]
    for dx, ref in enumerate((high_ref, own_ref, low_ref)):
        above, same, below = shifted([block_of(ref, g, ROWS) for g in range(GROUPS)])
        for dy, value in enumerate((below, same, above)):
            row = (dx * 3 + dy) * 128
            stack_ref[row : row + 128, :] = value
    terms = []
    for dz in range(3):
        left = jnp.concatenate([weight(weights_ref, core, k * 3 + dz) for k in range(9)], axis=1)
        terms.append(jnp.dot(left, stack_ref[...], preferred_element_type=F32))
    result_ref[...] = combine(terms[2], terms[1], terms[0]).reshape(GROUPS, 2, 16, CELLS)
    keep_ref[...] = result_ref[:, core]
    send_ref[...] = result_ref[:, 1 - core]


def forward_kernel(low_ref, own_ref, high_ref, other_ref, weights_ref, place_ref, out_ref, stack_ref):
    core = place_ref[0]
    first = core == 0
    for dx, ref in enumerate((low_ref, own_ref, high_ref)):
        pieces = []
        for g in range(GROUPS):
            mine = block_of(ref, g, 0)
            theirs = block_of(other_ref.at[dx], g, 0)
            pieces.append(jnp.where(first, mine, theirs))
            pieces.append(jnp.where(first, theirs, mine))
        for dy, value in enumerate(shifted(pieces)):
            row = (dx * 3 + dy) * 256
            stack_ref[row : row + 256, :] = value
    terms = []
    for dz in range(3):
        left = jnp.concatenate([weight(weights_ref, core, k * 3 + dz) for k in range(9)], axis=0)
        terms.append(
            lax.dot_general(left, stack_ref[...], (((0,), (0,)), ((), ())), preferred_element_type=F32)
        )
    out_ref[...] = combine(*terms).astype(BF16).reshape(GROUPS, 16, CELLS)


def merge_kernel(output_ref, keep_ref, got_ref, out_ref):
    out_ref[:, :16, :] = output_ref[...]
    out_ref[:, 16:, :] = (keep_ref[...] + got_ref[...]).astype(BF16)


def split_kernel(packed_ref, output_ref, grad_ref):
    for g in range(GROUPS):
        output_ref[:, g * CELLS : (g + 1) * CELLS] = packed_ref[g, :16, :]
        grad_ref[:, g * CELLS : (g + 1) * CELLS] = packed_ref[g, 16:, :]


def local(volume, filters, cotangent):
    swap = [(0, 1), (1, 0)]
    core = lax.axis_index("core").astype(jnp.int32)
    me = jnp.where(core == 0, lax.axis_index("y"), lax.axis_index("x")).astype(jnp.int32)
    place = jnp.stack([core, me])
    packed = run(
        pack_kernel,
        jax.ShapeDtypeStruct((GROUPS, 2 * ROWS + 16, 128), BF16),
        volume.reshape(16, 4096),
        cotangent.reshape(16, 4096),
        filters.reshape(OFFSETS, 16, 16),
    )
    packed = lax.all_to_all(packed, ("y", "zh"), 0, 0)
    own, weights = run(
        unpack_kernel,
        [
            jax.ShapeDtypeStruct((GROUPS, 2 * ROWS, 128), BF16),
            jax.ShapeDtypeStruct((4, PART, 16, 128), BF16),
        ],
        packed,
    )
    up = [(i, i + 1) for i in range(15)]
    down = [(b, a) for a, b in up]
    low = lax.ppermute(own, SPACE, up)
    high = lax.ppermute(own, SPACE, down)
    weights = lax.all_to_all(weights, "zl", 0, 0)
    weights = jnp.broadcast_to(weights, (4,) + weights.shape)
    mine = lax.all_to_all(weights, AXES, 0, 0, axis_index_groups=first_groups())
    last = lax.ppermute(mine, AXES, second_pairs(1))
    after = lax.ppermute(mine, AXES, second_pairs(3))
    far_a = lax.ppermute(last[:2], AXES, second_pairs(1))
    far_b = lax.ppermute(after[2:], AXES, second_pairs(3))
    other = lax.ppermute(jnp.stack([low[:, :ROWS], own[:, :ROWS], high[:, :ROWS]]), "core", swap)
    flops = 2 * 27 * 256 * 128 * CELLS
    piece = jax.ShapeDtypeStruct((GROUPS, 16, CELLS), F32)
    smem = pl.BlockSpec(memory_space=pltpu.SMEM)
    keep, send, weights = call(
        grad_kernel,
        [piece, piece, jax.ShapeDtypeStruct((4, 4, 4, PART, 16, 128), BF16)],
        flops=flops,
        byte_count=4 << 20,
        scratch=[pltpu.VMEM((9 * 128, CELLS), BF16), pltpu.VMEM((GROUPS, 2, 16, CELLS), F32)],
    )(in_specs=[VMEM] * 8 + [smem])(low, own, high, mine, after, last, far_a, far_b, place)
    got = lax.ppermute(send, "core", swap)
    output = call(
        forward_kernel,
        jax.ShapeDtypeStruct((GROUPS, 16, CELLS), BF16),
        flops=flops,
        byte_count=4 << 20,
        scratch=[pltpu.VMEM((9 * 256, CELLS), BF16)],
    )(in_specs=[VMEM] * 5 + [smem])(low, own, high, other, weights, place)
    merged = run(merge_kernel, jax.ShapeDtypeStruct((GROUPS, 32, CELLS), BF16), output, keep, got)
    merged = lax.all_to_all(merged, ("y", "zh"), 0, 0)
    plane = jax.ShapeDtypeStruct((16, 4096), BF16)
    output, grad = run(split_kernel, [plane, plane], merged)
    return output.reshape(16, 1, 4096), grad.reshape(16, 1, 4096)


def solution(mesh):
    split = Mesh(mesh.devices.reshape(4, 4, 4, 2, 2), AXES)
    act = P(FILT, SPACE, None)
    return jax.shard_map(
        local,
        mesh=split,
        in_specs=(act, P(None, None, None, SPACE, FILT), act),
        out_specs=(act, act),
        check_vma=False,
    )
```

```python
import functools
import itertools

import jax
import jax.numpy as jnp
from jax import lax
from jax.experimental import pallas as pl
from jax.experimental.pallas import tpu as pltpu
from jax.sharding import Mesh
from jax.sharding import PartitionSpec as P

AXES = ("zl", "x", "y", "zh", "core")
SPACE = ("zl", "x")
FILT = ("y", "zh", "core")
BF16 = jnp.bfloat16
F32 = jnp.float32
VMEM = pl.BlockSpec(memory_space=pltpu.VMEM)
PARAMS = pltpu.CompilerParams(vmem_limit_bytes=48 * 1024 * 1024)

GROUPS = 8
CELLS = 512
CHUNKS = 5
ROWS = CHUNKS * 16
OFFSETS = 27
PART = 7


def index_of(zl, x, y, zh, core):
    return (((zl * 4 + x) * 4 + y) * 2 + zh) * 2 + core


def everyone():
    return itertools.product(range(4), range(4), range(4), range(2), range(2))


def pairs_of(move):
    return [(index_of(*place), index_of(*move(*place))) for place in everyone()]


def along(first, step):
    def move(zl, x, y, zh, core):
        if (core == 0) == first:
            return zl, (x - step) % 4, y, zh, core
        return zl, x, (y - step) % 4, zh, core

    return pairs_of(move)


def call(kernel, out_shape, flops=0, byte_count=1 << 20, scratch=()):
    single = not isinstance(out_shape, (tuple, list))
    count = 1 if single else len(out_shape)
    return functools.partial(
        pl.pallas_call,
        kernel,
        out_shape=out_shape,
        out_specs=VMEM if single else [VMEM] * count,
        scratch_shapes=list(scratch),
        compiler_params=PARAMS,
        cost_estimate=pl.CostEstimate(flops=flops, bytes_accessed=byte_count, transcendentals=0),
    )


def run(kernel, out_shape, *args, **options):
    return call(kernel, out_shape, **options)(in_specs=[VMEM] * len(args))(*args)


def pack_kernel(place_ref, volume_ref, cotangent_ref, filters_ref, out_ref, weights_ref):
    zero = jnp.zeros((16, 16), BF16)
    for outer in range(PART):
        offsets = range(4 * outer, 4 * outer + 4)
        parts = [filters_ref[d] if d < OFFSETS else zero for d in offsets]

        @pl.when(place_ref[1] == 0)
        def _():
            weights_ref[outer] = jnp.concatenate([q for p in parts for q in (p, zero)], axis=1)

        @pl.when(place_ref[1] == 1)
        def _():
            weights_ref[outer] = jnp.concatenate([q for p in parts for q in (zero, p)], axis=1)

    lane = lax.broadcasted_iota(jnp.int32, (16, 128), 1)
    for part, ref in enumerate((volume_ref, cotangent_ref)):
        whole = pltpu.roll(ref[...].astype(F32), 64, 1)
        edge = whole[:, :128]
        pieces = [jnp.where(lane < 64, 0.0, edge)]
        pieces += [whole[:, 128 * j : 128 * (j + 1)] for j in range(1, 32)]
        pieces += [jnp.where(lane < 64, edge, 0.0)]
        pieces = [piece.astype(BF16) for piece in pieces]
        for slab in range(GROUPS):
            for chunk in range(CHUNKS):
                row = part * ROWS + chunk * 16
                out_ref[slab, row : row + 16, :] = pieces[4 * slab + chunk]


def shifted(pieces):
    whole = jnp.concatenate(pieces, axis=0)
    middle = pltpu.roll(whole.astype(F32), 640 - 64, 1).astype(BF16)
    return whole[:, :CELLS], middle[:, :CELLS], whole[:, 128:]


def block_of(ref, group, first):
    return jnp.concatenate(
        [ref[group, first + 16 * c : first + 16 * (c + 1), :] for c in range(CHUNKS)], axis=1
    )


def weight(weights_ref, d):
    return jnp.concatenate([weights_ref[s % 4, s // 4, d] for s in range(16)], axis=0)


def turned(value, by):
    return jnp.concatenate([value[:, 128 - by :], value[:, : 128 - by]], axis=1)


def assemble(place_ref, parts, held_ref, weights_ref):
    core, y, x, zl = place_ref[0], place_ref[2], place_ref[3], place_ref[4]
    for late, ref in enumerate(parts):
        for early in range(4):
            dy = jnp.where(core == 0, late, early)
            dx = jnp.where(core == 0, early, late)
            to_y, to_x = lax.rem(y + dy, 4), lax.rem(x + dx, 4)
            for k in range(4):
                held_ref[to_y, to_x, lax.rem(zl + k, 4)] = ref[early, k]
    lane = lax.broadcasted_iota(jnp.int32, (16, 128), 1)
    half, even = lane < 64, lane % 64 < 32
    for s in range(16):
        for outer in range(PART):
            a, b, c, d = (held_ref[k, s % 4, s // 4, outer] for k in range(4))
            a, c = jnp.where(half, a, turned(c, 64)), jnp.where(half, turned(a, 64), c)
            b, d = jnp.where(half, b, turned(d, 64)), jnp.where(half, turned(b, 64), d)
            weights_ref[s % 4, s // 4, 4 * outer] = jnp.where(even, a, turned(b, 32))
            weights_ref[s % 4, s // 4, 4 * outer + 1] = jnp.where(even, turned(a, 96), b)
            weights_ref[s % 4, s // 4, 4 * outer + 2] = jnp.where(even, c, turned(d, 32))
            weights_ref[s % 4, s // 4, 4 * outer + 3] = jnp.where(even, turned(c, 96), d)


def combine(before, middle, after):
    place = lax.broadcasted_iota(jnp.int32, middle.shape, 1) % 64
    left = jnp.where(place > 0, pltpu.roll(before, 1, 1), 0.0)
    right = jnp.where(place < 63, pltpu.roll(after, CELLS - 1, 1), 0.0)
    return middle + left + right


def grad_kernel(
    place_ref, low_ref, own_ref, high_ref, part_0, part_1, part_2, part_3,
    keep_ref, send_ref, weights_ref, held_ref, stack_ref, result_ref,
):
    assemble(place_ref, (part_0, part_1, part_2, part_3), held_ref, weights_ref)
    for dx, ref in enumerate((high_ref, own_ref, low_ref)):
        above, same, below = shifted([block_of(ref, g, ROWS) for g in range(GROUPS)])
        for dy, value in enumerate((below, same, above)):
            row = (dx * 3 + dy) * 128
            stack_ref[row : row + 128, :] = value
    terms = []
    for dz in range(3):
        left = jnp.concatenate([weight(weights_ref, k * 3 + dz) for k in range(9)], axis=1)
        terms.append(jnp.dot(left, stack_ref[...], preferred_element_type=F32))
    result_ref[...] = combine(terms[2], terms[1], terms[0]).reshape(GROUPS, 2, 16, CELLS)
    core = place_ref[0]
    keep_ref[...] = result_ref[:, core]
    send_ref[...] = result_ref[:, 1 - core]


def forward_kernel(place_ref, low_ref, own_ref, high_ref, other_ref, weights_ref, out_ref, stack_ref):
    first = place_ref[0] == 0
    for dx, ref in enumerate((low_ref, own_ref, high_ref)):
        pieces = []
        for g in range(GROUPS):
            mine = block_of(ref, g, 0)
            theirs = block_of(other_ref.at[dx], g, 0)
            pieces.append(jnp.where(first, mine, theirs))
            pieces.append(jnp.where(first, theirs, mine))
        for dy, value in enumerate(shifted(pieces)):
            row = (dx * 3 + dy) * 256
            stack_ref[row : row + 256, :] = value
    terms = []
    for dz in range(3):
        left = jnp.concatenate([weight(weights_ref, k * 3 + dz) for k in range(9)], axis=0)
        terms.append(
            lax.dot_general(left, stack_ref[...], (((0,), (0,)), ((), ())), preferred_element_type=F32)
        )
    out_ref[...] = combine(*terms).astype(BF16).reshape(GROUPS, 16, CELLS)


def merge_kernel(output_ref, keep_ref, got_ref, out_ref):
    out_ref[:, :16, :] = output_ref[...]
    out_ref[:, 16:, :] = (keep_ref[...] + got_ref[...]).astype(BF16)


def split_kernel(packed_ref, output_ref, grad_ref):
    for g in range(GROUPS):
        output_ref[:, g * CELLS : (g + 1) * CELLS] = packed_ref[g, :16, :]
        grad_ref[:, g * CELLS : (g + 1) * CELLS] = packed_ref[g, 16:, :]


def local(volume, filters, cotangent):
    swap = [(0, 1), (1, 0)]
    place = jnp.stack([lax.axis_index(name) for name in ("core", "zh", "y", "x", "zl")]).astype(jnp.int32)
    smem = pl.BlockSpec(memory_space=pltpu.SMEM)
    own, unit = call(
        pack_kernel,
        [
            jax.ShapeDtypeStruct((GROUPS, 2 * ROWS, 128), BF16),
            jax.ShapeDtypeStruct((PART, 16, 128), BF16),
        ],
    )(in_specs=[smem] + [VMEM] * 3)(
        place,
        volume.reshape(16, 4096),
        cotangent.reshape(16, 4096),
        filters.reshape(OFFSETS, 16, 16),
    )
    unit = unit + lax.ppermute(unit, "zh", swap)
    own = lax.all_to_all(own, ("y", "zh"), 0, 0)

    def gather(block, pairs):
        return [block] + [lax.ppermute(block, AXES, pairs(step)) for step in (1, 2, 3)]

    def line(step):
        return pairs_of(lambda zl, x, y, zh, core: ((zl - step) % 4, x, y, zh, core))

    unit = jnp.stack(gather(unit, line))
    unit = jnp.stack(gather(unit, functools.partial(along, True)))
    parts = gather(unit, functools.partial(along, False))
    up = [(i, i + 1) for i in range(15)]
    down = [(b, a) for a, b in up]
    low = lax.ppermute(own, SPACE, up)
    high = lax.ppermute(own, SPACE, down)
    other = lax.ppermute(jnp.stack([low[:, :ROWS], own[:, :ROWS], high[:, :ROWS]]), "core", swap)
    flops = 2 * 27 * 256 * 128 * CELLS
    piece = jax.ShapeDtypeStruct((GROUPS, 16, CELLS), F32)
    keep, send, weights = call(
        grad_kernel,
        [piece, piece, jax.ShapeDtypeStruct((4, 4, 4 * PART, 16, 128), BF16)],
        flops=flops,
        byte_count=4 << 20,
        scratch=[
            pltpu.VMEM((4, 4, 4, PART, 16, 128), BF16),
            pltpu.VMEM((9 * 128, CELLS), BF16),
            pltpu.VMEM((GROUPS, 2, 16, CELLS), F32),
        ],
    )(in_specs=[smem] + [VMEM] * 7)(place, low, own, high, *parts)
    got = lax.ppermute(send, "core", swap)
    output = call(
        forward_kernel,
        jax.ShapeDtypeStruct((GROUPS, 16, CELLS), BF16),
        flops=flops,
        byte_count=4 << 20,
        scratch=[pltpu.VMEM((9 * 256, CELLS), BF16)],
    )(in_specs=[smem] + [VMEM] * 5)(place, low, own, high, other, weights)
    merged = run(merge_kernel, jax.ShapeDtypeStruct((GROUPS, 32, CELLS), BF16), output, keep, got)
    merged = lax.all_to_all(merged, ("y", "zh"), 0, 0)
    plane = jax.ShapeDtypeStruct((16, 4096), BF16)
    output, grad = run(split_kernel, [plane, plane], merged)
    return output.reshape(16, 1, 4096), grad.reshape(16, 1, 4096)


def solution(mesh):
    split = Mesh(mesh.devices.reshape(4, 4, 4, 2, 2), AXES)
    act = P(FILT, SPACE, None)
    return jax.shard_map(
        local,
        mesh=split,
        in_specs=(act, P(None, None, None, SPACE, FILT), act),
        out_specs=(act, act),
        check_vma=False,
    )
```

```python
import functools
import itertools

import jax
import jax.numpy as jnp
from jax import lax
from jax.experimental import pallas as pl
from jax.experimental.pallas import tpu as pltpu
from jax.sharding import Mesh
from jax.sharding import PartitionSpec as P

AXES = ("zl", "x", "y", "zh", "core")
SPACE = ("zl", "x")
FILT = ("y", "zh", "core")
BF16 = jnp.bfloat16
F32 = jnp.float32
VMEM = pl.BlockSpec(memory_space=pltpu.VMEM)
PARAMS = pltpu.CompilerParams(vmem_limit_bytes=48 * 1024 * 1024)

GROUPS = 8
CELLS = 512
CHUNKS = 5
ROWS = CHUNKS * 16
OFFSETS = 27
PART = 7


def index_of(zl, x, y, zh, core):
    return (((zl * 4 + x) * 4 + y) * 2 + zh) * 2 + core


def everyone():
    return itertools.product(range(4), range(4), range(4), range(2), range(2))


def pairs_of(move):
    return [(index_of(*place), index_of(*move(*place))) for place in everyone()]


def along(first, step):
    def move(zl, x, y, zh, core):
        if (core == 0) == first:
            return zl, (x - step) % 4, y, zh, core
        return zl, x, (y - step) % 4, zh, core

    return pairs_of(move)


def call(kernel, out_shape, flops=0, byte_count=1 << 20, scratch=()):
    single = not isinstance(out_shape, (tuple, list))
    count = 1 if single else len(out_shape)
    return functools.partial(
        pl.pallas_call,
        kernel,
        out_shape=out_shape,
        out_specs=VMEM if single else [VMEM] * count,
        scratch_shapes=list(scratch),
        compiler_params=PARAMS,
        cost_estimate=pl.CostEstimate(flops=flops, bytes_accessed=byte_count, transcendentals=0),
    )


def run(kernel, out_shape, *args, **options):
    return call(kernel, out_shape, **options)(in_specs=[VMEM] * len(args))(*args)


def pack_filters_kernel(filters_ref, out_ref):
    zero = jnp.zeros((16, 16), BF16)
    for outer in range(4):
        offsets = range(8 * outer, 8 * outer + 8)
        block = jnp.concatenate([filters_ref[d] if d < OFFSETS else zero for d in offsets], axis=1)
        for copy in range(8):
            out_ref[copy, outer] = block


def regroup_kernel(packed_ref, out_ref):
    for zl in range(4):
        for outer in range(PART):
            pieces = []
            for d in range(4 * outer, 4 * outer + 4):
                lane = 16 * (d % 8)
                pieces += [packed_ref[2 * zl + zh, d // 8, :, lane : lane + 16] for zh in range(2)]
            out_ref[zl, outer] = jnp.concatenate(pieces, axis=1)


def pack_kernel(volume_ref, cotangent_ref, out_ref):
    lane = lax.broadcasted_iota(jnp.int32, (16, 128), 1)
    for part, ref in enumerate((volume_ref, cotangent_ref)):
        whole = pltpu.roll(ref[...].astype(F32), 64, 1)
        edge = whole[:, :128]
        pieces = [jnp.where(lane < 64, 0.0, edge)]
        pieces += [whole[:, 128 * j : 128 * (j + 1)] for j in range(1, 32)]
        pieces += [jnp.where(lane < 64, edge, 0.0)]
        pieces = [piece.astype(BF16) for piece in pieces]
        for slab in range(GROUPS):
            for chunk in range(CHUNKS):
                row = part * ROWS + chunk * 16
                out_ref[slab, row : row + 16, :] = pieces[4 * slab + chunk]


def shifted(pieces):
    whole = jnp.concatenate(pieces, axis=0)
    middle = pltpu.roll(whole.astype(F32), 640 - 64, 1).astype(BF16)
    return whole[:, :CELLS], middle[:, :CELLS], whole[:, 128:]


def block_of(ref, group, first):
    return jnp.concatenate(
        [ref[group, first + 16 * c : first + 16 * (c + 1), :] for c in range(CHUNKS)], axis=1
    )


def weight(weights_ref, d):
    return jnp.concatenate([weights_ref[s % 4, s // 4, d] for s in range(16)], axis=0)


def turned(value, by):
    return jnp.concatenate([value[:, 128 - by :], value[:, : 128 - by]], axis=1)


def assemble_kernel(part_0, part_1, part_2, part_3, weights_ref, held_ref):
    core, y, x = (lax.axis_index(name) for name in ("core", "y", "x"))
    for late, ref in enumerate((part_0, part_1, part_2, part_3)):
        for early in range(4):
            dy = jnp.where(core == 0, late, early)
            dx = jnp.where(core == 0, early, late)
            held_ref[lax.rem(y + dy, 4), lax.rem(x + dx, 4)] = ref[early]
    lane = lax.broadcasted_iota(jnp.int32, (16, 128), 1)
    half, even = lane < 64, lane % 64 < 32
    for s in range(16):
        for outer in range(PART):
            a, b, c, d = (held_ref[k, s % 4, s // 4, outer] for k in range(4))
            a, c = jnp.where(half, a, turned(c, 64)), jnp.where(half, turned(a, 64), c)
            b, d = jnp.where(half, b, turned(d, 64)), jnp.where(half, turned(b, 64), d)
            weights_ref[s % 4, s // 4, 4 * outer] = jnp.where(even, a, turned(b, 32))
            weights_ref[s % 4, s // 4, 4 * outer + 1] = jnp.where(even, turned(a, 96), b)
            weights_ref[s % 4, s // 4, 4 * outer + 2] = jnp.where(even, c, turned(d, 32))
            weights_ref[s % 4, s // 4, 4 * outer + 3] = jnp.where(even, turned(c, 96), d)


def combine(before, middle, after):
    place = lax.broadcasted_iota(jnp.int32, middle.shape, 1) % 64
    left = jnp.where(place > 0, pltpu.roll(before, 1, 1), 0.0)
    right = jnp.where(place < 63, pltpu.roll(after, CELLS - 1, 1), 0.0)
    return middle + left + right


def grad_kernel(low_ref, own_ref, high_ref, weights_ref, keep_ref, send_ref, stack_ref, result_ref):
    for dx, ref in enumerate((high_ref, own_ref, low_ref)):
        above, same, below = shifted([block_of(ref, g, ROWS) for g in range(GROUPS)])
        for dy, value in enumerate((below, same, above)):
            row = (dx * 3 + dy) * 128
            stack_ref[row : row + 128, :] = value
    terms = []
    for dz in range(3):
        left = jnp.concatenate([weight(weights_ref, k * 3 + dz) for k in range(9)], axis=1)
        terms.append(jnp.dot(left, stack_ref[...], preferred_element_type=F32))
    result_ref[...] = combine(terms[2], terms[1], terms[0]).reshape(GROUPS, 2, 16, CELLS)
    core = lax.axis_index("core")
    keep_ref[...] = result_ref[:, core]
    send_ref[...] = result_ref[:, 1 - core]


def forward_kernel(low_ref, own_ref, high_ref, other_ref, weights_ref, out_ref, stack_ref):
    first = lax.axis_index("core") == 0
    for dx, ref in enumerate((low_ref, own_ref, high_ref)):
        pieces = []
        for g in range(GROUPS):
            mine = block_of(ref, g, 0)
            theirs = block_of(other_ref.at[dx], g, 0)
            pieces.append(jnp.where(first, mine, theirs))
            pieces.append(jnp.where(first, theirs, mine))
        for dy, value in enumerate(shifted(pieces)):
            row = (dx * 3 + dy) * 256
            stack_ref[row : row + 256, :] = value
    terms = []
    for dz in range(3):
        left = jnp.concatenate([weight(weights_ref, k * 3 + dz) for k in range(9)], axis=0)
        terms.append(
            lax.dot_general(left, stack_ref[...], (((0,), (0,)), ((), ())), preferred_element_type=F32)
        )
    out_ref[...] = combine(*terms).astype(BF16).reshape(GROUPS, 16, CELLS)


def merge_kernel(output_ref, keep_ref, got_ref, out_ref):
    out_ref[:, :16, :] = output_ref[...]
    out_ref[:, 16:, :] = (keep_ref[...] + got_ref[...]).astype(BF16)


def split_kernel(packed_ref, output_ref, grad_ref):
    for g in range(GROUPS):
        output_ref[:, g * CELLS : (g + 1) * CELLS] = packed_ref[g, :16, :]
        grad_ref[:, g * CELLS : (g + 1) * CELLS] = packed_ref[g, 16:, :]


def local(volume, filters, cotangent):
    swap = [(0, 1), (1, 0)]
    packed = run(
        pack_filters_kernel,
        jax.ShapeDtypeStruct((8, 4, 16, 128), BF16),
        filters.reshape(OFFSETS, 16, 16),
    )
    packed = lax.all_to_all(packed, ("zl", "zh"), 0, 0)
    own = run(
        pack_kernel,
        jax.ShapeDtypeStruct((GROUPS, 2 * ROWS, 128), BF16),
        volume.reshape(16, 4096),
        cotangent.reshape(16, 4096),
    )
    own, packed = lax.optimization_barrier((own, packed))
    own = lax.all_to_all(own, ("y", "zh"), 0, 0)
    unit = run(regroup_kernel, jax.ShapeDtypeStruct((4, PART, 16, 128), BF16), packed)

    def gather(block, pairs):
        return [block] + [lax.ppermute(block, AXES, pairs(step)) for step in (1, 2, 3)]

    unit = jnp.stack(gather(unit, functools.partial(along, True)))
    own, _ = lax.optimization_barrier((own, unit))
    parts = gather(unit, functools.partial(along, False))
    up = [(i, i + 1) for i in range(15)]
    down = [(b, a) for a, b in up]
    low = lax.ppermute(own, SPACE, up)
    high = lax.ppermute(own, SPACE, down)
    other = lax.ppermute(jnp.stack([low[:, :ROWS], own[:, :ROWS], high[:, :ROWS]]), "core", swap)
    flops = 2 * 27 * 256 * 128 * CELLS
    piece = jax.ShapeDtypeStruct((GROUPS, 16, CELLS), F32)
    weights = run(
        assemble_kernel,
        jax.ShapeDtypeStruct((4, 4, 4 * PART, 16, 128), BF16),
        *parts,
        byte_count=8 << 20,
        scratch=[pltpu.VMEM((4, 4, 4, PART, 16, 128), BF16)],
    )
    keep, send = run(
        grad_kernel,
        [piece, piece],
        low,
        own,
        high,
        weights,
        flops=flops,
        byte_count=4 << 20,
        scratch=[pltpu.VMEM((9 * 128, CELLS), BF16), pltpu.VMEM((GROUPS, 2, 16, CELLS), F32)],
    )
    got = lax.ppermute(send, "core", swap)
    output = run(
        forward_kernel,
        jax.ShapeDtypeStruct((GROUPS, 16, CELLS), BF16),
        low,
        own,
        high,
        other,
        weights,
        flops=flops,
        byte_count=4 << 20,
        scratch=[pltpu.VMEM((9 * 256, CELLS), BF16)],
    )
    merged = run(merge_kernel, jax.ShapeDtypeStruct((GROUPS, 32, CELLS), BF16), output, keep, got)
    merged = lax.all_to_all(merged, ("y", "zh"), 0, 0)
    plane = jax.ShapeDtypeStruct((16, 4096), BF16)
    output, grad = run(split_kernel, [plane, plane], merged)
    return output.reshape(16, 1, 4096), grad.reshape(16, 1, 4096)


def solution(mesh):
    split = Mesh(mesh.devices.reshape(4, 4, 4, 2, 2), AXES)
    act = P(FILT, SPACE, None)
    return jax.shard_map(
        local,
        mesh=split,
        in_specs=(act, P(None, None, None, SPACE, FILT), act),
        out_specs=(act, act),
        check_vma=False,
    )
```

```python
import functools
import itertools

import jax
import jax.numpy as jnp
from jax import lax
from jax.experimental import pallas as pl
from jax.experimental.pallas import tpu as pltpu
from jax.sharding import Mesh
from jax.sharding import PartitionSpec as P

AXES = ("zl", "x", "y", "zh", "core")
SPACE = ("zl", "x")
FILT = ("y", "zh", "core")
BF16 = jnp.bfloat16
F32 = jnp.float32
VMEM = pl.BlockSpec(memory_space=pltpu.VMEM)

GROUPS = 8
CELLS = 512
CHUNKS = 5
ROWS = CHUNKS * 16
OFFSETS = 27
PART = 7


def index_of(zl, x, y, zh, core):
    return (((zl * 4 + x) * 4 + y) * 2 + zh) * 2 + core


def everyone():
    return itertools.product(range(4), range(4), range(4), range(2), range(2))


def pairs_of(move):
    return [(index_of(*place), index_of(*move(*place))) for place in everyone()]


def along(first, step):
    def move(zl, x, y, zh, core):
        if (core == 0) == first:
            return zl, (x - step) % 4, y, zh, core
        return zl, x, (y - step) % 4, zh, core

    return pairs_of(move)


def call(kernel, out_shape, flops=0, byte_count=1 << 20, scratch=(), mib=48):
    single = not isinstance(out_shape, (tuple, list))
    count = 1 if single else len(out_shape)
    return functools.partial(
        pl.pallas_call,
        kernel,
        out_shape=out_shape,
        out_specs=VMEM if single else [VMEM] * count,
        scratch_shapes=list(scratch),
        compiler_params=pltpu.CompilerParams(vmem_limit_bytes=mib << 20),
        cost_estimate=pl.CostEstimate(flops=flops, bytes_accessed=byte_count, transcendentals=0),
    )


def run(kernel, out_shape, *args, **options):
    return call(kernel, out_shape, **options)(in_specs=[VMEM] * len(args))(*args)


def pack_kernel(
    volume_ref, cotangent_ref, filters_ref, packed_ref, keep_ref, send_ref,
    volume, cotangent, filters, slabs_ref, sems,
):
    pairs = ((filters_ref, filters), (volume_ref, volume), (cotangent_ref, cotangent))
    copies = [pltpu.make_async_copy(a, b, sems.at[k]) for k, (a, b) in enumerate(pairs)]
    for copy in copies:
        copy.start()
    copies[0].wait()
    zero = jnp.zeros((16, 16), BF16)
    for outer in range(4):
        offsets = range(8 * outer, 8 * outer + 8)
        block = jnp.concatenate([filters[d] if d < OFFSETS else zero for d in offsets], axis=1)
        for copy in range(8):
            packed_ref[copy, outer] = block
    lane = lax.broadcasted_iota(jnp.int32, (16, 128), 1)
    for part, ref in enumerate((volume, cotangent)):
        copies[1 + part].wait()
        whole = pltpu.roll(ref[...].astype(F32), 64, 1)
        edge = whole[:, :128]
        pieces = [jnp.where(lane < 64, 0.0, edge)]
        pieces += [whole[:, 128 * j : 128 * (j + 1)] for j in range(1, 32)]
        pieces += [jnp.where(lane < 64, edge, 0.0)]
        pieces = [piece.astype(BF16) for piece in pieces]
        for slab in range(GROUPS):
            for chunk in range(CHUNKS):
                row = part * ROWS + chunk * 16
                slabs_ref[slab, row : row + 16, :] = pieces[4 * slab + chunk]
    zh = lax.axis_index("zh")
    for y in range(4):
        keep_ref[y] = slabs_ref[2 * y + zh]
        send_ref[y] = slabs_ref[2 * y + 1 - zh]


def route_kernel(keep_ref, got_ref, *out_refs):
    y, zh = lax.axis_index("y"), lax.axis_index("zh")
    for step, ref in enumerate(out_refs):
        to = lax.rem(y + 4 - step, 4)
        ref[zh] = keep_ref[to]
        ref[1 - zh] = got_ref[to]


def regroup_kernel(packed_ref, out_ref):
    for zl in range(4):
        for outer in range(PART):
            pieces = []
            for d in range(4 * outer, 4 * outer + 4):
                lane = 16 * (d % 8)
                pieces += [packed_ref[2 * zl + zh, d // 8, :, lane : lane + 16] for zh in range(2)]
            out_ref[zl, outer] = jnp.concatenate(pieces, axis=1)


def shifted(pieces):
    whole = jnp.concatenate(pieces, axis=0)
    middle = pltpu.roll(whole.astype(F32), 640 - 64, 1).astype(BF16)
    return whole[:, :CELLS], middle[:, :CELLS], whole[:, 128:]


def block_of(ref, group, first):
    return jnp.concatenate(
        [ref[group, first + 16 * c : first + 16 * (c + 1), :] for c in range(CHUNKS)], axis=1
    )


def turned(value, by):
    return jnp.concatenate([value[:, 128 - by :], value[:, : 128 - by]], axis=1)


def assemble(parts, weights_ref):
    lane = lax.broadcasted_iota(jnp.int32, (16, 128), 1)
    half, even = lane < 64, lane % 64 < 32

    def turn(pick):
        for zl in range(4):
            for x in range(4):
                row = 16 * (4 * zl + x)
                for outer in range(PART):
                    a, b, c, d = (pick(y, x)[zl, outer] for y in range(4))
                    a, c = jnp.where(half, a, turned(c, 64)), jnp.where(half, turned(a, 64), c)
                    b, d = jnp.where(half, b, turned(d, 64)), jnp.where(half, turned(b, 64), d)
                    for k, value in enumerate((
                        jnp.where(even, a, turned(b, 32)),
                        jnp.where(even, turned(a, 96), b),
                        jnp.where(even, c, turned(d, 32)),
                        jnp.where(even, turned(c, 96), d),
                    )):
                        weights_ref[4 * outer + k, row : row + 16, :] = value

    @pl.when(lax.axis_index("core") == 0)
    def _():
        turn(lambda y, x: parts[y].at[x])

    @pl.when(lax.axis_index("core") == 1)
    def _():
        turn(lambda y, x: parts[x].at[y])


def combine(before, middle, after):
    place = lax.broadcasted_iota(jnp.int32, middle.shape, 1) % 64
    left = jnp.where(place > 0, pltpu.roll(before, 1, 1), 0.0)
    right = jnp.where(place < 63, pltpu.roll(after, CELLS - 1, 1), 0.0)
    return middle + left + right


def grad_kernel(
    low_ref, own_ref, high_ref, part_0, part_1, part_2, part_3,
    keep_ref, send_ref, weights_ref, stack_ref, result_ref,
):
    assemble((part_0, part_1, part_2, part_3), weights_ref)
    for dx, ref in enumerate((high_ref, own_ref, low_ref)):
        above, same, below = shifted([block_of(ref, g, ROWS) for g in range(GROUPS)])
        for dy, value in enumerate((below, same, above)):
            row = (dx * 3 + dy) * 128
            stack_ref[row : row + 128, :] = value
    terms = []
    for dz in range(3):
        left = jnp.concatenate([weights_ref[k * 3 + dz] for k in range(9)], axis=1)
        terms.append(jnp.dot(left, stack_ref[...], preferred_element_type=F32))
    total = combine(terms[2], terms[1], terms[0])
    core, my_x = lax.axis_index("core"), lax.axis_index("x")
    for zl in range(4):
        for step in range(4):
            x = lax.rem(my_x + step, 4)
            row = 16 * (4 * zl + step)
            result_ref[2 * zl + x // 2, lax.rem(x, 2)] = total[row : row + 16]
    keep_ref[...] = result_ref[:, core]
    send_ref[...] = result_ref[:, 1 - core]


def forward_kernel(low_ref, own_ref, high_ref, other_ref, weights_ref, out_ref, volume_ref, stack_ref):
    core, my_x, my_y = (lax.axis_index(name) for name in ("core", "x", "y"))
    for dx, ref in enumerate((low_ref, own_ref, high_ref)):
        for g in range(GROUPS):
            volume_ref[dx, 2 * g + core] = block_of(ref, g, 0)
            volume_ref[dx, 2 * g + 1 - core] = block_of(other_ref.at[dx], g, 0)
        pieces = []
        for zl in range(4):
            for step in range(4):
                x = lax.rem(my_x + step, 4)
                pieces.append(volume_ref[dx, 4 * lax.rem(zl + 4 - my_y, 4) + x])
        for dy, value in enumerate(shifted(pieces)):
            row = (dx * 3 + dy) * 256
            stack_ref[row : row + 256, :] = value
    terms = []
    for dz in range(3):
        left = jnp.concatenate([weights_ref[k * 3 + dz] for k in range(9)], axis=0)
        terms.append(
            lax.dot_general(left, stack_ref[...], (((0,), (0,)), ((), ())), preferred_element_type=F32)
        )
    total = combine(*terms).astype(BF16)
    for step in range(4):
        y = lax.rem(my_y + step, 4)
        for zh in range(2):
            row = 16 * (2 * step + zh)
            out_ref[2 * y + zh] = total[row : row + 16]


def merge_kernel(output_ref, keep_ref, got_ref, out_ref):
    out_ref[:, :16, :] = output_ref[...]
    out_ref[:, 16:, :] = (keep_ref[...] + got_ref[...]).astype(BF16)


def split_kernel(packed_ref, output_ref, grad_ref):
    for g in range(GROUPS):
        output_ref[:, g * CELLS : (g + 1) * CELLS] = packed_ref[g, :16, :]
        grad_ref[:, g * CELLS : (g + 1) * CELLS] = packed_ref[g, 16:, :]


def local(volume, filters, cotangent):
    swap = [(0, 1), (1, 0)]
    half = jax.ShapeDtypeStruct((4, 2 * ROWS, 128), BF16)
    packed, keep, send = call(
        pack_kernel,
        [jax.ShapeDtypeStruct((8, 4, 16, 128), BF16), half, half],
        scratch=[
            pltpu.VMEM((16, 4096), BF16),
            pltpu.VMEM((16, 4096), BF16),
            pltpu.VMEM((OFFSETS, 16, 16), BF16),
            pltpu.VMEM((GROUPS, 2 * ROWS, 128), BF16),
            pltpu.SemaphoreType.DMA((3,)),
        ],
        mib=60,
    )(in_specs=[pl.BlockSpec(memory_space=pl.ANY)] * 3)(
        volume.reshape(16, 4096),
        cotangent.reshape(16, 4096),
        filters.reshape(OFFSETS, 16, 16),
    )
    got = lax.ppermute(send, "zh", swap)
    packed = lax.all_to_all(packed, ("zl", "zh"), 0, 0)
    routed = run(route_kernel, [jax.ShapeDtypeStruct((2, 2 * ROWS, 128), BF16)] * 4, keep, got)
    own = [routed[0]]
    for step in (1, 2, 3):
        own.append(lax.ppermute(routed[step], "y", [(i, (i - step) % 4) for i in range(4)]))
    own = jnp.stack(own).reshape(GROUPS, 2 * ROWS, 128)
    unit = run(regroup_kernel, jax.ShapeDtypeStruct((4, PART, 16, 128), BF16), packed)

    def gather(block, pairs):
        return [block] + [lax.ppermute(block, AXES, pairs(step)) for step in (1, 2, 3)]

    unit = jnp.stack(gather(unit, functools.partial(along, True)))
    parts = gather(unit, functools.partial(along, False))
    up = [(i, i + 1) for i in range(15)]
    down = [(b, a) for a, b in up]
    low = lax.ppermute(own, SPACE, up)
    high = lax.ppermute(own, SPACE, down)
    other = lax.ppermute(jnp.stack([low[:, :ROWS], own[:, :ROWS], high[:, :ROWS]]), "core", swap)
    flops = 2 * 27 * 256 * 128 * CELLS
    piece = jax.ShapeDtypeStruct((GROUPS, 16, CELLS), F32)
    keep, send, weights = run(
        grad_kernel,
        [piece, piece, jax.ShapeDtypeStruct((4 * PART, 256, 128), BF16)],
        low,
        own,
        high,
        *parts,
        flops=flops,
        byte_count=4 << 20,
        scratch=[pltpu.VMEM((9 * 128, CELLS), BF16), pltpu.VMEM((GROUPS, 2, 16, CELLS), F32)],
    )
    got = lax.ppermute(send, "core", swap)
    output = run(
        forward_kernel,
        jax.ShapeDtypeStruct((GROUPS, 16, CELLS), BF16),
        low,
        own,
        high,
        other,
        weights,
        flops=flops,
        byte_count=4 << 20,
        scratch=[
            pltpu.VMEM((3, 16, 16, CHUNKS * 128), BF16),
            pltpu.VMEM((9 * 256, CELLS), BF16),
        ],
    )
    merged = run(merge_kernel, jax.ShapeDtypeStruct((GROUPS, 32, CELLS), BF16), output, keep, got)
    merged = lax.all_to_all(merged, ("y", "zh"), 0, 0)
    plane = jax.ShapeDtypeStruct((16, 4096), BF16)
    output, grad = run(split_kernel, [plane, plane], merged)
    return output.reshape(16, 1, 4096), grad.reshape(16, 1, 4096)


def solution(mesh):
    split = Mesh(mesh.devices.reshape(4, 4, 4, 2, 2), AXES)
    act = P(FILT, SPACE, None)
    return jax.shard_map(
        local,
        mesh=split,
        in_specs=(act, P(None, None, None, SPACE, FILT), act),
        out_specs=(act, act),
        check_vma=False,
    )
```

```python
import functools
import itertools

import jax
import jax.numpy as jnp
from jax import lax
from jax.experimental import pallas as pl
from jax.experimental.pallas import tpu as pltpu
from jax.sharding import Mesh
from jax.sharding import PartitionSpec as P

AXES = ("zl", "x", "y", "zh", "core")
SPACE = ("zl", "x")
FILT = ("y", "zh", "core")
BF16 = jnp.bfloat16
F32 = jnp.float32
VMEM = pl.BlockSpec(memory_space=pltpu.VMEM)

GROUPS = 8
CELLS = 512
CHUNKS = 5
ROWS = CHUNKS * 16
OFFSETS = 27
PART = 7


def index_of(zl, x, y, zh, core):
    return (((zl * 4 + x) * 4 + y) * 2 + zh) * 2 + core


def everyone():
    return itertools.product(range(4), range(4), range(4), range(2), range(2))


def pairs_of(move):
    return [(index_of(*place), index_of(*move(*place))) for place in everyone()]


def along(first, step):
    def move(zl, x, y, zh, core):
        if (core == 0) == first:
            return zl, (x - step) % 4, y, zh, core
        return zl, x, (y - step) % 4, zh, core

    return pairs_of(move)


def call(kernel, out_shape, flops=0, byte_count=1 << 20, scratch=(), mib=48):
    single = not isinstance(out_shape, (tuple, list))
    count = 1 if single else len(out_shape)
    return functools.partial(
        pl.pallas_call,
        kernel,
        out_shape=out_shape,
        out_specs=VMEM if single else [VMEM] * count,
        scratch_shapes=list(scratch),
        compiler_params=pltpu.CompilerParams(vmem_limit_bytes=mib << 20),
        cost_estimate=pl.CostEstimate(flops=flops, bytes_accessed=byte_count, transcendentals=0),
    )


def run(kernel, out_shape, *args, **options):
    return call(kernel, out_shape, **options)(in_specs=[VMEM] * len(args))(*args)


def pack_kernel(
    volume_ref, cotangent_ref, filters_ref, packed_ref, keep_ref, send_ref,
    volume, cotangent, filters, slabs_ref, sems,
):
    pairs = ((filters_ref, filters), (volume_ref, volume), (cotangent_ref, cotangent))
    copies = [pltpu.make_async_copy(a, b, sems.at[k]) for k, (a, b) in enumerate(pairs)]
    for copy in copies:
        copy.start()
    copies[0].wait()
    zero = jnp.zeros((16, 16), BF16)
    for outer in range(4):
        offsets = range(8 * outer, 8 * outer + 8)
        block = jnp.concatenate([filters[d] if d < OFFSETS else zero for d in offsets], axis=1)
        for copy in range(8):
            packed_ref[copy, outer] = block
    lane = lax.broadcasted_iota(jnp.int32, (16, 128), 1)
    for part, ref in enumerate((volume, cotangent)):
        copies[1 + part].wait()
        whole = pltpu.roll(ref[...].astype(F32), 64, 1)
        edge = whole[:, :128]
        pieces = [jnp.where(lane < 64, 0.0, edge)]
        pieces += [whole[:, 128 * j : 128 * (j + 1)] for j in range(1, 32)]
        pieces += [jnp.where(lane < 64, edge, 0.0)]
        pieces = [piece.astype(BF16) for piece in pieces]
        for slab in range(GROUPS):
            for chunk in range(CHUNKS):
                row = part * ROWS + chunk * 16
                slabs_ref[slab, row : row + 16, :] = pieces[4 * slab + chunk]
    zh = lax.axis_index("zh")
    for y in range(4):
        keep_ref[y] = slabs_ref[2 * y + zh]
        send_ref[y] = slabs_ref[2 * y + 1 - zh]


def route_kernel(keep_ref, got_ref, *out_refs):
    y, zh = lax.axis_index("y"), lax.axis_index("zh")
    for step, ref in enumerate(out_refs):
        to = lax.rem(y + 4 - step, 4)
        ref[zh] = keep_ref[to]
        ref[1 - zh] = got_ref[to]


def regroup_kernel(packed_ref, out_ref):
    for zl in range(4):
        for outer in range(PART):
            pieces = []
            for d in range(4 * outer, 4 * outer + 4):
                lane = 16 * (d % 8)
                pieces += [packed_ref[2 * zl + zh, d // 8, :, lane : lane + 16] for zh in range(2)]
            out_ref[zl, outer] = jnp.concatenate(pieces, axis=1)


def shifted(pieces):
    whole = jnp.concatenate(pieces, axis=0)
    middle = pltpu.roll(whole.astype(F32), 640 - 64, 1).astype(BF16)
    return whole[:, :CELLS], middle[:, :CELLS], whole[:, 128:]


def block_of(ref, group, first):
    return jnp.concatenate(
        [ref[group, first + 16 * c : first + 16 * (c + 1), :] for c in range(CHUNKS)], axis=1
    )


def turned(value, by):
    return jnp.concatenate([value[:, 128 - by :], value[:, : 128 - by]], axis=1)


def assemble(parts, weights_ref):
    lane = lax.broadcasted_iota(jnp.int32, (PART * 16, 128), 1)
    half, even = lane < 64, lane % 64 < 32

    def turn(pick):
        for zl in range(4):
            for x in range(4):
                row = 16 * (4 * zl + x)
                a, b, c, d = (pick(y, x)[zl].reshape(PART * 16, 128) for y in range(4))
                a, c = jnp.where(half, a, turned(c, 64)), jnp.where(half, turned(a, 64), c)
                b, d = jnp.where(half, b, turned(d, 64)), jnp.where(half, turned(b, 64), d)
                values = (
                    jnp.where(even, a, turned(b, 32)),
                    jnp.where(even, turned(a, 96), b),
                    jnp.where(even, c, turned(d, 32)),
                    jnp.where(even, turned(c, 96), d),
                )
                for outer in range(PART):
                    for k, value in enumerate(values):
                        weights_ref[4 * outer + k, row : row + 16, :] = value[16 * outer : 16 * (outer + 1)]

    @pl.when(lax.axis_index("core") == 0)
    def _():
        turn(lambda y, x: parts[y].at[x])

    @pl.when(lax.axis_index("core") == 1)
    def _():
        turn(lambda y, x: parts[x].at[y])


def combine(before, middle, after):
    place = lax.broadcasted_iota(jnp.int32, middle.shape, 1) % 64
    left = jnp.where(place > 0, pltpu.roll(before, 1, 1), 0.0)
    right = jnp.where(place < 63, pltpu.roll(after, CELLS - 1, 1), 0.0)
    return middle + left + right


def grad_kernel(
    low_ref, own_ref, high_ref, part_0, part_1, part_2, part_3,
    keep_ref, send_ref, weights_ref, stack_ref, result_ref,
):
    assemble((part_0, part_1, part_2, part_3), weights_ref)
    for dx, ref in enumerate((high_ref, own_ref, low_ref)):
        above, same, below = shifted([block_of(ref, g, ROWS) for g in range(GROUPS)])
        for dy, value in enumerate((below, same, above)):
            row = (dx * 3 + dy) * 128
            stack_ref[row : row + 128, :] = value
    terms = []
    for dz in range(3):
        left = jnp.concatenate([weights_ref[k * 3 + dz] for k in range(9)], axis=1)
        terms.append(jnp.dot(left, stack_ref[...], preferred_element_type=F32))
    total = combine(terms[2], terms[1], terms[0])
    core, my_x = lax.axis_index("core"), lax.axis_index("x")
    for zl in range(4):
        for step in range(4):
            x = lax.rem(my_x + step, 4)
            row = 16 * (4 * zl + step)
            result_ref[2 * zl + x // 2, lax.rem(x, 2)] = total[row : row + 16]
    keep_ref[...] = result_ref[:, core]
    send_ref[...] = result_ref[:, 1 - core]


def forward_kernel(low_ref, own_ref, high_ref, other_ref, weights_ref, out_ref, volume_ref, stack_ref):
    core, my_x, my_y = (lax.axis_index(name) for name in ("core", "x", "y"))
    for dx, ref in enumerate((low_ref, own_ref, high_ref)):
        for g in range(GROUPS):
            volume_ref[dx, 2 * g + core] = block_of(ref, g, 0)
            volume_ref[dx, 2 * g + 1 - core] = block_of(other_ref.at[dx], g, 0)
        pieces = []
        for zl in range(4):
            for step in range(4):
                x = lax.rem(my_x + step, 4)
                pieces.append(volume_ref[dx, 4 * lax.rem(zl + 4 - my_y, 4) + x])
        for dy, value in enumerate(shifted(pieces)):
            row = (dx * 3 + dy) * 256
            stack_ref[row : row + 256, :] = value
    terms = []
    for dz in range(3):
        left = jnp.concatenate([weights_ref[k * 3 + dz] for k in range(9)], axis=0)
        terms.append(
            lax.dot_general(left, stack_ref[...], (((0,), (0,)), ((), ())), preferred_element_type=F32)
        )
    total = combine(*terms).astype(BF16)
    for step in range(4):
        y = lax.rem(my_y + step, 4)
        for zh in range(2):
            row = 16 * (2 * step + zh)
            out_ref[2 * y + zh] = total[row : row + 16]


def merge_kernel(output_ref, keep_ref, got_ref, out_ref):
    out_ref[:, :16, :] = output_ref[...]
    out_ref[:, 16:, :] = (keep_ref[...] + got_ref[...]).astype(BF16)


def split_kernel(packed_ref, output_ref, grad_ref):
    for g in range(GROUPS):
        output_ref[:, g * CELLS : (g + 1) * CELLS] = packed_ref[g, :16, :]
        grad_ref[:, g * CELLS : (g + 1) * CELLS] = packed_ref[g, 16:, :]


def local(volume, filters, cotangent):
    swap = [(0, 1), (1, 0)]
    half = jax.ShapeDtypeStruct((4, 2 * ROWS, 128), BF16)
    packed, keep, send = call(
        pack_kernel,
        [jax.ShapeDtypeStruct((8, 4, 16, 128), BF16), half, half],
        scratch=[
            pltpu.VMEM((16, 4096), BF16),
            pltpu.VMEM((16, 4096), BF16),
            pltpu.VMEM((OFFSETS, 16, 16), BF16),
            pltpu.VMEM((GROUPS, 2 * ROWS, 128), BF16),
            pltpu.SemaphoreType.DMA((3,)),
        ],
        mib=60,
    )(in_specs=[pl.BlockSpec(memory_space=pl.ANY)] * 3)(
        volume.reshape(16, 4096),
        cotangent.reshape(16, 4096),
        filters.reshape(OFFSETS, 16, 16),
    )
    got = lax.ppermute(send, "zh", swap)
    packed = lax.all_to_all(packed, ("zl", "zh"), 0, 0)
    routed = run(route_kernel, [jax.ShapeDtypeStruct((2, 2 * ROWS, 128), BF16)] * 4, keep, got)
    own = [routed[0]]
    for step in (1, 2, 3):
        own.append(lax.ppermute(routed[step], "y", [(i, (i - step) % 4) for i in range(4)]))
    own = jnp.stack(own).reshape(GROUPS, 2 * ROWS, 128)
    unit = run(regroup_kernel, jax.ShapeDtypeStruct((4, PART, 16, 128), BF16), packed)

    def gather(block, pairs):
        return [block] + [lax.ppermute(block, AXES, pairs(step)) for step in (1, 2, 3)]

    unit = jnp.stack(gather(unit, functools.partial(along, True)))
    parts = gather(unit, functools.partial(along, False))
    up = [(i, i + 1) for i in range(15)]
    down = [(b, a) for a, b in up]
    low = lax.ppermute(own, SPACE, up)
    high = lax.ppermute(own, SPACE, down)
    other = lax.ppermute(jnp.stack([low[:, :ROWS], own[:, :ROWS], high[:, :ROWS]]), "core", swap)
    flops = 2 * 27 * 256 * 128 * CELLS
    piece = jax.ShapeDtypeStruct((GROUPS, 16, CELLS), F32)
    keep, send, weights = run(
        grad_kernel,
        [piece, piece, jax.ShapeDtypeStruct((4 * PART, 256, 128), BF16)],
        low,
        own,
        high,
        *parts,
        flops=flops,
        byte_count=4 << 20,
        scratch=[pltpu.VMEM((9 * 128, CELLS), BF16), pltpu.VMEM((GROUPS, 2, 16, CELLS), F32)],
    )
    got = lax.ppermute(send, "core", swap)
    output = run(
        forward_kernel,
        jax.ShapeDtypeStruct((GROUPS, 16, CELLS), BF16),
        low,
        own,
        high,
        other,
        weights,
        flops=flops,
        byte_count=4 << 20,
        scratch=[
            pltpu.VMEM((3, 16, 16, CHUNKS * 128), BF16),
            pltpu.VMEM((9 * 256, CELLS), BF16),
        ],
    )
    merged = run(merge_kernel, jax.ShapeDtypeStruct((GROUPS, 32, CELLS), BF16), output, keep, got)
    merged = lax.all_to_all(merged, ("y", "zh"), 0, 0)
    plane = jax.ShapeDtypeStruct((16, 4096), BF16)
    output, grad = run(split_kernel, [plane, plane], merged)
    return output.reshape(16, 1, 4096), grad.reshape(16, 1, 4096)


def solution(mesh):
    split = Mesh(mesh.devices.reshape(4, 4, 4, 2, 2), AXES)
    act = P(FILT, SPACE, None)
    return jax.shard_map(
        local,
        mesh=split,
        in_specs=(act, P(None, None, None, SPACE, FILT), act),
        out_specs=(act, act),
        check_vma=False,
    )
```

```python
import functools
import itertools

import jax
import jax.numpy as jnp
from jax import lax
from jax.experimental import pallas as pl
from jax.experimental.pallas import tpu as pltpu
from jax.sharding import Mesh
from jax.sharding import PartitionSpec as P

AXES = ("zl", "x", "y", "zh", "core")
SPACE = ("zl", "x")
FILT = ("y", "zh", "core")
BF16 = jnp.bfloat16
F32 = jnp.float32
VMEM = pl.BlockSpec(memory_space=pltpu.VMEM)

GROUPS = 8
CELLS = 512
CHUNKS = 5
ROWS = CHUNKS * 16
OFFSETS = 27
PART = 7


def index_of(zl, x, y, zh, core):
    return (((zl * 4 + x) * 4 + y) * 2 + zh) * 2 + core


def everyone():
    return itertools.product(range(4), range(4), range(4), range(2), range(2))


def pairs_of(move):
    return [(index_of(*place), index_of(*move(*place))) for place in everyone()]


def along(first, step):
    def move(zl, x, y, zh, core):
        if (core == 0) == first:
            return zl, (x - step) % 4, y, zh, core
        return zl, x, (y - step) % 4, zh, core

    return pairs_of(move)


def call(kernel, out_shape, flops=0, byte_count=1 << 20, scratch=(), mib=48):
    single = not isinstance(out_shape, (tuple, list))
    count = 1 if single else len(out_shape)
    return functools.partial(
        pl.pallas_call,
        kernel,
        out_shape=out_shape,
        out_specs=VMEM if single else [VMEM] * count,
        scratch_shapes=list(scratch),
        compiler_params=pltpu.CompilerParams(vmem_limit_bytes=mib << 20),
        cost_estimate=pl.CostEstimate(flops=flops, bytes_accessed=byte_count, transcendentals=0),
    )


def run(kernel, out_shape, *args, **options):
    return call(kernel, out_shape, **options)(in_specs=[VMEM] * len(args))(*args)


def pack_kernel(
    volume_ref, cotangent_ref, filters_ref, packed_ref, keep_ref, send_ref,
    volume, cotangent, filters, slabs_ref, sems,
):
    pairs = ((filters_ref, filters), (volume_ref, volume), (cotangent_ref, cotangent))
    copies = [pltpu.make_async_copy(a, b, sems.at[k]) for k, (a, b) in enumerate(pairs)]
    for copy in copies:
        copy.start()
    copies[0].wait()
    zero = jnp.zeros((16, 16), BF16)
    for outer in range(4):
        offsets = range(8 * outer, 8 * outer + 8)
        block = jnp.concatenate([filters[d] if d < OFFSETS else zero for d in offsets], axis=1)
        for copy in range(8):
            packed_ref[copy, outer] = block
    lane = lax.broadcasted_iota(jnp.int32, (16, 128), 1)
    for part, ref in enumerate((volume, cotangent)):
        copies[1 + part].wait()
        whole = pltpu.roll(ref[...].astype(F32), 64, 1)
        edge = whole[:, :128]
        pieces = [jnp.where(lane < 64, 0.0, edge)]
        pieces += [whole[:, 128 * j : 128 * (j + 1)] for j in range(1, 32)]
        pieces += [jnp.where(lane < 64, edge, 0.0)]
        pieces = [piece.astype(BF16) for piece in pieces]
        for slab in range(GROUPS):
            for chunk in range(CHUNKS):
                row = part * ROWS + chunk * 16
                slabs_ref[slab, row : row + 16, :] = pieces[4 * slab + chunk]
    zh = lax.axis_index("zh")
    for y in range(4):
        keep_ref[y] = slabs_ref[2 * y + zh]
        send_ref[y] = slabs_ref[2 * y + 1 - zh]


def route_kernel(keep_ref, got_ref, *out_refs):
    y, zh = lax.axis_index("y"), lax.axis_index("zh")
    for step, ref in enumerate(out_refs):
        to = lax.rem(y + 4 - step, 4)
        ref[zh] = keep_ref[to]
        ref[1 - zh] = got_ref[to]


def regroup_kernel(packed_ref, out_ref):
    for zl in range(4):
        for outer in range(PART):
            pieces = []
            for d in range(4 * outer, 4 * outer + 4):
                lane = 16 * (d % 8)
                pieces += [packed_ref[2 * zl + zh, d // 8, :, lane : lane + 16] for zh in range(2)]
            out_ref[zl, outer] = jnp.concatenate(pieces, axis=1)


def stack_kernel(part_0, part_1, part_2, part_3, out_ref):
    for k, ref in enumerate((part_0, part_1, part_2, part_3)):
        out_ref[2 * k : 2 * k + 2] = ref[...]


def shifted(pieces):
    whole = jnp.concatenate(pieces, axis=0)
    middle = pltpu.roll(whole.astype(F32), 640 - 64, 1).astype(BF16)
    return whole[:, :CELLS], middle[:, :CELLS], whole[:, 128:]


def block_of(ref, group, first):
    return jnp.concatenate(
        [ref[group, first + 16 * c : first + 16 * (c + 1), :] for c in range(CHUNKS)], axis=1
    )


def turned(value, by):
    return jnp.concatenate([value[:, 128 - by :], value[:, : 128 - by]], axis=1)


def assemble(parts, first_ref, weights_ref):
    lane = lax.broadcasted_iota(jnp.int32, (PART * 16, 128), 1)
    half, even = lane < 64, lane % 64 < 32

    def block(late, early):
        if late == 1:
            return first_ref if early == 3 else parts[1].at[early]
        return parts[late].at[early]

    def turn(pick):
        for zl in range(4):
            for x in range(4):
                row = 16 * (4 * zl + x)
                a, b, c, d = (pick(y, x)[zl].reshape(PART * 16, 128) for y in range(4))
                a, c = jnp.where(half, a, turned(c, 64)), jnp.where(half, turned(a, 64), c)
                b, d = jnp.where(half, b, turned(d, 64)), jnp.where(half, turned(b, 64), d)
                values = (
                    jnp.where(even, a, turned(b, 32)),
                    jnp.where(even, turned(a, 96), b),
                    jnp.where(even, c, turned(d, 32)),
                    jnp.where(even, turned(c, 96), d),
                )
                for outer in range(PART):
                    for k, value in enumerate(values):
                        weights_ref[4 * outer + k, row : row + 16, :] = value[16 * outer : 16 * (outer + 1)]

    @pl.when(lax.axis_index("core") == 0)
    def _():
        turn(lambda y, x: block(y, x))

    @pl.when(lax.axis_index("core") == 1)
    def _():
        turn(lambda y, x: block(x, y))


def combine(before, middle, after):
    place = lax.broadcasted_iota(jnp.int32, middle.shape, 1) % 64
    left = jnp.where(place > 0, pltpu.roll(before, 1, 1), 0.0)
    right = jnp.where(place < 63, pltpu.roll(after, CELLS - 1, 1), 0.0)
    return middle + left + right


def grad_kernel(
    low_ref, own_ref, high_ref, part_0, first_ref, part_1, part_2, part_3,
    keep_ref, send_ref, weights_ref, stack_ref, result_ref,
):
    assemble((part_0, part_1, part_2, part_3), first_ref, weights_ref)
    for dx, ref in enumerate((high_ref, own_ref, low_ref)):
        above, same, below = shifted([block_of(ref, g, ROWS) for g in range(GROUPS)])
        for dy, value in enumerate((below, same, above)):
            row = (dx * 3 + dy) * 128
            stack_ref[row : row + 128, :] = value
    terms = []
    for dz in range(3):
        left = jnp.concatenate([weights_ref[k * 3 + dz] for k in range(9)], axis=1)
        terms.append(jnp.dot(left, stack_ref[...], preferred_element_type=F32))
    total = combine(terms[2], terms[1], terms[0])
    core, my_x = lax.axis_index("core"), lax.axis_index("x")
    for zl in range(4):
        for step in range(4):
            x = lax.rem(my_x + step, 4)
            row = 16 * (4 * zl + step)
            result_ref[2 * zl + x // 2, lax.rem(x, 2)] = total[row : row + 16]
    keep_ref[...] = result_ref[:, core]
    send_ref[...] = result_ref[:, 1 - core]


def forward_kernel(low_ref, own_ref, high_ref, other_ref, weights_ref, out_ref, volume_ref, stack_ref):
    core, my_x, my_y = (lax.axis_index(name) for name in ("core", "x", "y"))
    for dx, ref in enumerate((low_ref, own_ref, high_ref)):
        for g in range(GROUPS):
            volume_ref[dx, 2 * g + core] = block_of(ref, g, 0)
            volume_ref[dx, 2 * g + 1 - core] = block_of(other_ref.at[dx], g, 0)
        pieces = []
        for zl in range(4):
            for step in range(4):
                x = lax.rem(my_x + step, 4)
                pieces.append(volume_ref[dx, 4 * lax.rem(zl + 4 - my_y, 4) + x])
        for dy, value in enumerate(shifted(pieces)):
            row = (dx * 3 + dy) * 256
            stack_ref[row : row + 256, :] = value
    terms = []
    for dz in range(3):
        left = jnp.concatenate([weights_ref[k * 3 + dz] for k in range(9)], axis=0)
        terms.append(
            lax.dot_general(left, stack_ref[...], (((0,), (0,)), ((), ())), preferred_element_type=F32)
        )
    total = combine(*terms).astype(BF16)
    for step in range(4):
        y = lax.rem(my_y + step, 4)
        for zh in range(2):
            row = 16 * (2 * step + zh)
            out_ref[2 * y + zh] = total[row : row + 16]


def merge_kernel(output_ref, keep_ref, got_ref, out_ref):
    out_ref[:, :16, :] = output_ref[...]
    out_ref[:, 16:, :] = (keep_ref[...] + got_ref[...]).astype(BF16)


def split_kernel(packed_ref, output_ref, grad_ref):
    for g in range(GROUPS):
        output_ref[:, g * CELLS : (g + 1) * CELLS] = packed_ref[g, :16, :]
        grad_ref[:, g * CELLS : (g + 1) * CELLS] = packed_ref[g, 16:, :]


def local(volume, filters, cotangent):
    swap = [(0, 1), (1, 0)]
    half = jax.ShapeDtypeStruct((4, 2 * ROWS, 128), BF16)
    packed, keep, send = call(
        pack_kernel,
        [jax.ShapeDtypeStruct((8, 4, 16, 128), BF16), half, half],
        scratch=[
            pltpu.VMEM((16, 4096), BF16),
            pltpu.VMEM((16, 4096), BF16),
            pltpu.VMEM((OFFSETS, 16, 16), BF16),
            pltpu.VMEM((GROUPS, 2 * ROWS, 128), BF16),
            pltpu.SemaphoreType.DMA((3,)),
        ],
        mib=60,
    )(in_specs=[pl.BlockSpec(memory_space=pl.ANY)] * 3)(
        volume.reshape(16, 4096),
        cotangent.reshape(16, 4096),
        filters.reshape(OFFSETS, 16, 16),
    )
    got = lax.ppermute(send, "zh", swap)
    packed = lax.all_to_all(packed, ("zl", "zh"), 0, 0)
    routed = run(route_kernel, [jax.ShapeDtypeStruct((2, 2 * ROWS, 128), BF16)] * 4, keep, got)
    own = [routed[0]]
    for step in (1, 2, 3):
        own.append(lax.ppermute(routed[step], "y", [(i, (i - step) % 4) for i in range(4)]))
    unit = run(regroup_kernel, jax.ShapeDtypeStruct((4, PART, 16, 128), BF16), packed)

    def gather(block, pairs):
        return [block] + [lax.ppermute(block, AXES, pairs(step)) for step in (1, 2, 3)]

    unit = jnp.stack(gather(unit, functools.partial(along, True)))
    parts = [unit]
    for step in (1, 2, 3):
        pairs = along(False, step)
        if step == 1:
            first = lax.ppermute(unit[3], AXES, pairs)
            *own, first = lax.optimization_barrier((*own, first))
            parts += [first, lax.ppermute(unit[:3], AXES, pairs)]
        else:
            parts.append(lax.ppermute(unit, AXES, pairs))
    own = run(
        stack_kernel,
        jax.ShapeDtypeStruct((GROUPS, 2 * ROWS, 128), BF16),
        *own,
        byte_count=32 << 20,
    )
    up = [(i, i + 1) for i in range(15)]
    down = [(b, a) for a, b in up]
    low = lax.ppermute(own, SPACE, up)
    high = lax.ppermute(own, SPACE, down)
    other = lax.ppermute(jnp.stack([low[:, :ROWS], own[:, :ROWS], high[:, :ROWS]]), "core", swap)
    flops = 2 * 27 * 256 * 128 * CELLS
    piece = jax.ShapeDtypeStruct((GROUPS, 16, CELLS), F32)
    keep, send, weights = run(
        grad_kernel,
        [piece, piece, jax.ShapeDtypeStruct((4 * PART, 256, 128), BF16)],
        low,
        own,
        high,
        *parts,
        flops=flops,
        byte_count=4 << 20,
        scratch=[pltpu.VMEM((9 * 128, CELLS), BF16), pltpu.VMEM((GROUPS, 2, 16, CELLS), F32)],
    )
    got = lax.ppermute(send, "core", swap)
    output = run(
        forward_kernel,
        jax.ShapeDtypeStruct((GROUPS, 16, CELLS), BF16),
        low,
        own,
        high,
        other,
        weights,
        flops=flops,
        byte_count=4 << 20,
        scratch=[
            pltpu.VMEM((3, 16, 16, CHUNKS * 128), BF16),
            pltpu.VMEM((9 * 256, CELLS), BF16),
        ],
    )
    merged = run(merge_kernel, jax.ShapeDtypeStruct((GROUPS, 32, CELLS), BF16), output, keep, got)
    merged = lax.all_to_all(merged, ("y", "zh"), 0, 0)
    plane = jax.ShapeDtypeStruct((16, 4096), BF16)
    output, grad = run(split_kernel, [plane, plane], merged)
    return output.reshape(16, 1, 4096), grad.reshape(16, 1, 4096)


def solution(mesh):
    split = Mesh(mesh.devices.reshape(4, 4, 4, 2, 2), AXES)
    act = P(FILT, SPACE, None)
    return jax.shard_map(
        local,
        mesh=split,
        in_specs=(act, P(None, None, None, SPACE, FILT), act),
        out_specs=(act, act),
        check_vma=False,
    )
```

```python
import functools
import itertools

import jax
import jax.numpy as jnp
from jax import lax
from jax.experimental import pallas as pl
from jax.experimental.pallas import tpu as pltpu
from jax.sharding import Mesh
from jax.sharding import PartitionSpec as P

AXES = ("zl", "x", "y", "zh", "core")
SPACE = ("zl", "x")
FILT = ("y", "zh", "core")
BF16 = jnp.bfloat16
F32 = jnp.float32
VMEM = pl.BlockSpec(memory_space=pltpu.VMEM)

GROUPS = 8
CELLS = 512
CHUNKS = 5
ROWS = CHUNKS * 16
OFFSETS = 27
PART = 7


def index_of(zl, x, y, zh, core):
    return (((zl * 4 + x) * 4 + y) * 2 + zh) * 2 + core


def everyone():
    return itertools.product(range(4), range(4), range(4), range(2), range(2))


def pairs_of(move):
    return [(index_of(*place), index_of(*move(*place))) for place in everyone()]


def along(first, step):
    def move(zl, x, y, zh, core):
        if (core == 0) == first:
            return zl, (x - step) % 4, y, zh, core
        return zl, x, (y - step) % 4, zh, core

    return pairs_of(move)


def call(kernel, out_shape, flops=0, byte_count=1 << 20, scratch=(), mib=48):
    single = not isinstance(out_shape, (tuple, list))
    count = 1 if single else len(out_shape)
    return functools.partial(
        pl.pallas_call,
        kernel,
        out_shape=out_shape,
        out_specs=VMEM if single else [VMEM] * count,
        scratch_shapes=list(scratch),
        compiler_params=pltpu.CompilerParams(vmem_limit_bytes=mib << 20),
        cost_estimate=pl.CostEstimate(flops=flops, bytes_accessed=byte_count, transcendentals=0),
    )


def run(kernel, out_shape, *args, **options):
    return call(kernel, out_shape, **options)(in_specs=[VMEM] * len(args))(*args)


def pack_kernel(
    volume_ref, cotangent_ref, filters_ref, packed_ref, send_ref,
    volume, cotangent, filters, slabs_ref, sems,
):
    pairs = ((filters_ref, filters), (volume_ref, volume), (cotangent_ref, cotangent))
    copies = [pltpu.make_async_copy(a, b, sems.at[k]) for k, (a, b) in enumerate(pairs)]
    for copy in copies:
        copy.start()
    copies[0].wait()
    zero = jnp.zeros((16, 16), BF16)
    for outer in range(4):
        offsets = range(8 * outer, 8 * outer + 8)
        block = jnp.concatenate([filters[d] if d < OFFSETS else zero for d in offsets], axis=1)
        for copy in range(8):
            packed_ref[copy, outer] = block
    lane = lax.broadcasted_iota(jnp.int32, (16, 128), 1)
    for part, ref in enumerate((volume, cotangent)):
        copies[1 + part].wait()
        whole = pltpu.roll(ref[...].astype(F32), 64, 1)
        edge = whole[:, :128]
        pieces = [jnp.where(lane < 64, 0.0, edge)]
        pieces += [whole[:, 128 * j : 128 * (j + 1)] for j in range(1, 32)]
        pieces += [jnp.where(lane < 64, edge, 0.0)]
        pieces = [piece.astype(BF16) for piece in pieces]
        for slab in range(GROUPS):
            for chunk in range(CHUNKS):
                row = part * ROWS + chunk * 16
                slabs_ref[slab, row : row + 16, :] = pieces[4 * slab + chunk]
    zh = lax.axis_index("zh")
    for y in range(4):
        send_ref[y] = slabs_ref[2 * y + 1 - zh]


def keep_kernel(volume, cotangent, keep_ref, slabs_ref):
    lane = lax.broadcasted_iota(jnp.int32, (16, 128), 1)
    for part, ref in enumerate((volume, cotangent)):
        whole = pltpu.roll(ref[...].astype(F32), 64, 1)
        edge = whole[:, :128]
        pieces = [jnp.where(lane < 64, 0.0, edge)]
        pieces += [whole[:, 128 * j : 128 * (j + 1)] for j in range(1, 32)]
        pieces += [jnp.where(lane < 64, edge, 0.0)]
        pieces = [piece.astype(BF16) for piece in pieces]
        for slab in range(GROUPS):
            for chunk in range(CHUNKS):
                row = part * ROWS + chunk * 16
                slabs_ref[slab, row : row + 16, :] = pieces[4 * slab + chunk]
    zh = lax.axis_index("zh")
    for y in range(4):
        keep_ref[y] = slabs_ref[2 * y + zh]


def route_kernel(keep_ref, got_ref, *out_refs):
    y, zh = lax.axis_index("y"), lax.axis_index("zh")
    for step, ref in enumerate(out_refs):
        to = lax.rem(y + 4 - step, 4)
        ref[zh] = keep_ref[to]
        ref[1 - zh] = got_ref[to]


def regroup_kernel(packed_ref, out_ref):
    for zl in range(4):
        for outer in range(PART):
            pieces = []
            for d in range(4 * outer, 4 * outer + 4):
                lane = 16 * (d % 8)
                pieces += [packed_ref[2 * zl + zh, d // 8, :, lane : lane + 16] for zh in range(2)]
            out_ref[zl, outer] = jnp.concatenate(pieces, axis=1)


def shifted(pieces):
    whole = jnp.concatenate(pieces, axis=0)
    middle = pltpu.roll(whole.astype(F32), 640 - 64, 1).astype(BF16)
    return whole[:, :CELLS], middle[:, :CELLS], whole[:, 128:]


def block_of(ref, group, first):
    return jnp.concatenate(
        [ref[group, first + 16 * c : first + 16 * (c + 1), :] for c in range(CHUNKS)], axis=1
    )


def turned(value, by):
    return jnp.concatenate([value[:, 128 - by :], value[:, : 128 - by]], axis=1)


def assemble(parts, weights_ref):
    lane = lax.broadcasted_iota(jnp.int32, (PART * 16, 128), 1)
    half, even = lane < 64, lane % 64 < 32

    def turn(pick):
        for zl in range(4):
            for x in range(4):
                row = 16 * (4 * zl + x)
                a, b, c, d = (pick(y, x)[zl].reshape(PART * 16, 128) for y in range(4))
                a, c = jnp.where(half, a, turned(c, 64)), jnp.where(half, turned(a, 64), c)
                b, d = jnp.where(half, b, turned(d, 64)), jnp.where(half, turned(b, 64), d)
                values = (
                    jnp.where(even, a, turned(b, 32)),
                    jnp.where(even, turned(a, 96), b),
                    jnp.where(even, c, turned(d, 32)),
                    jnp.where(even, turned(c, 96), d),
                )
                for outer in range(PART):
                    for k, value in enumerate(values):
                        weights_ref[4 * outer + k, row : row + 16, :] = value[16 * outer : 16 * (outer + 1)]

    @pl.when(lax.axis_index("core") == 0)
    def _():
        turn(lambda y, x: parts[y].at[x])

    @pl.when(lax.axis_index("core") == 1)
    def _():
        turn(lambda y, x: parts[x].at[y])


def combine(before, middle, after):
    place = lax.broadcasted_iota(jnp.int32, middle.shape, 1) % 64
    left = jnp.where(place > 0, pltpu.roll(before, 1, 1), 0.0)
    right = jnp.where(place < 63, pltpu.roll(after, CELLS - 1, 1), 0.0)
    return middle + left + right


def assemble_kernel(part_0, part_1, part_2, part_3, weights_ref):
    assemble((part_0, part_1, part_2, part_3), weights_ref)


def grad_kernel(
    low_ref, own_ref, high_ref, weights_ref, keep_ref, send_ref, stack_ref, result_ref,
):
    for dx, ref in enumerate((high_ref, own_ref, low_ref)):
        above, same, below = shifted([block_of(ref, g, ROWS) for g in range(GROUPS)])
        for dy, value in enumerate((below, same, above)):
            row = (dx * 3 + dy) * 128
            stack_ref[row : row + 128, :] = value
    terms = []
    for dz in range(3):
        left = jnp.concatenate([weights_ref[k * 3 + dz] for k in range(9)], axis=1)
        terms.append(jnp.dot(left, stack_ref[...], preferred_element_type=F32))
    total = combine(terms[2], terms[1], terms[0])
    core, my_x = lax.axis_index("core"), lax.axis_index("x")
    for zl in range(4):
        for step in range(4):
            x = lax.rem(my_x + step, 4)
            row = 16 * (4 * zl + step)
            result_ref[2 * zl + x // 2, lax.rem(x, 2)] = total[row : row + 16]
    keep_ref[...] = result_ref[:, core]
    send_ref[...] = result_ref[:, 1 - core]


def forward_kernel(low_ref, own_ref, high_ref, other_ref, weights_ref, out_ref, volume_ref, stack_ref):
    core, my_x, my_y = (lax.axis_index(name) for name in ("core", "x", "y"))
    for dx, ref in enumerate((low_ref, own_ref, high_ref)):
        for g in range(GROUPS):
            volume_ref[dx, 2 * g + core] = block_of(ref, g, 0)
            volume_ref[dx, 2 * g + 1 - core] = block_of(other_ref.at[dx], g, 0)
        pieces = []
        for zl in range(4):
            for step in range(4):
                x = lax.rem(my_x + step, 4)
                pieces.append(volume_ref[dx, 4 * lax.rem(zl + 4 - my_y, 4) + x])
        for dy, value in enumerate(shifted(pieces)):
            row = (dx * 3 + dy) * 256
            stack_ref[row : row + 256, :] = value
    terms = []
    for dz in range(3):
        left = jnp.concatenate([weights_ref[k * 3 + dz] for k in range(9)], axis=0)
        terms.append(
            lax.dot_general(left, stack_ref[...], (((0,), (0,)), ((), ())), preferred_element_type=F32)
        )
    total = combine(*terms).astype(BF16)
    for step in range(4):
        y = lax.rem(my_y + step, 4)
        for zh in range(2):
            row = 16 * (2 * step + zh)
            out_ref[2 * y + zh] = total[row : row + 16]


def merge_kernel(output_ref, keep_ref, got_ref, out_ref):
    out_ref[:, :16, :] = output_ref[...]
    out_ref[:, 16:, :] = (keep_ref[...] + got_ref[...]).astype(BF16)


def split_kernel(packed_ref, output_ref, grad_ref):
    for g in range(GROUPS):
        output_ref[:, g * CELLS : (g + 1) * CELLS] = packed_ref[g, :16, :]
        grad_ref[:, g * CELLS : (g + 1) * CELLS] = packed_ref[g, 16:, :]


def local(volume, filters, cotangent):
    swap = [(0, 1), (1, 0)]
    half = jax.ShapeDtypeStruct((4, 2 * ROWS, 128), BF16)
    packed, send = call(
        pack_kernel,
        [jax.ShapeDtypeStruct((8, 4, 16, 128), BF16), half],
        scratch=[
            pltpu.VMEM((16, 4096), BF16),
            pltpu.VMEM((16, 4096), BF16),
            pltpu.VMEM((OFFSETS, 16, 16), BF16),
            pltpu.VMEM((GROUPS, 2 * ROWS, 128), BF16),
            pltpu.SemaphoreType.DMA((3,)),
        ],
        mib=60,
    )(in_specs=[pl.BlockSpec(memory_space=pl.ANY)] * 3)(
        volume.reshape(16, 4096),
        cotangent.reshape(16, 4096),
        filters.reshape(OFFSETS, 16, 16),
    )
    got = lax.ppermute(send, "zh", swap)
    keep = run(
        keep_kernel,
        half,
        volume.reshape(16, 4096),
        cotangent.reshape(16, 4096),
        scratch=[pltpu.VMEM((GROUPS, 2 * ROWS, 128), BF16)],
    )
    packed = lax.all_to_all(packed, ("zl", "zh"), 0, 0)
    routed = run(route_kernel, [jax.ShapeDtypeStruct((2, 2 * ROWS, 128), BF16)] * 4, keep, got)
    own = [routed[0]]
    for step in (1, 2, 3):
        own.append(lax.ppermute(routed[step], "y", [(i, (i - step) % 4) for i in range(4)]))
    own = jnp.stack(own).reshape(GROUPS, 2 * ROWS, 128)
    unit = run(regroup_kernel, jax.ShapeDtypeStruct((4, PART, 16, 128), BF16), packed)

    def gather(block, pairs):
        return [block] + [lax.ppermute(block, AXES, pairs(step)) for step in (1, 2, 3)]

    unit = jnp.stack(gather(unit, functools.partial(along, True)))
    own, _ = lax.optimization_barrier((own, unit))
    parts = gather(unit, functools.partial(along, False))
    up = [(i, i + 1) for i in range(15)]
    down = [(b, a) for a, b in up]
    low = lax.ppermute(own, SPACE, up)
    high = lax.ppermute(own, SPACE, down)
    other = lax.ppermute(jnp.stack([low[:, :ROWS], own[:, :ROWS], high[:, :ROWS]]), "core", swap)
    flops = 2 * 27 * 256 * 128 * CELLS
    piece = jax.ShapeDtypeStruct((GROUPS, 16, CELLS), F32)
    weights = run(
        assemble_kernel,
        jax.ShapeDtypeStruct((4 * PART, 256, 128), BF16),
        *parts,
        byte_count=64 << 20,
    )
    keep, send = run(
        grad_kernel,
        [piece, piece],
        low,
        own,
        high,
        weights,
        flops=flops,
        byte_count=4 << 20,
        scratch=[pltpu.VMEM((9 * 128, CELLS), BF16), pltpu.VMEM((GROUPS, 2, 16, CELLS), F32)],
    )
    got = lax.ppermute(send, "core", swap)
    output = run(
        forward_kernel,
        jax.ShapeDtypeStruct((GROUPS, 16, CELLS), BF16),
        low,
        own,
        high,
        other,
        weights,
        flops=flops,
        byte_count=4 << 20,
        scratch=[
            pltpu.VMEM((3, 16, 16, CHUNKS * 128), BF16),
            pltpu.VMEM((9 * 256, CELLS), BF16),
        ],
    )
    merged = run(merge_kernel, jax.ShapeDtypeStruct((GROUPS, 32, CELLS), BF16), output, keep, got)
    merged = lax.all_to_all(merged, ("y", "zh"), 0, 0)
    plane = jax.ShapeDtypeStruct((16, 4096), BF16)
    output, grad = run(split_kernel, [plane, plane], merged)
    return output.reshape(16, 1, 4096), grad.reshape(16, 1, 4096)


def solution(mesh):
    split = Mesh(mesh.devices.reshape(4, 4, 4, 2, 2), AXES)
    act = P(FILT, SPACE, None)
    return jax.shard_map(
        local,
        mesh=split,
        in_specs=(act, P(None, None, None, SPACE, FILT), act),
        out_specs=(act, act),
        check_vma=False,
    )
```

```python
import functools
import itertools

import jax
import jax.numpy as jnp
from jax import lax
from jax.experimental import pallas as pl
from jax.experimental.pallas import tpu as pltpu
from jax.sharding import Mesh
from jax.sharding import PartitionSpec as P

AXES = ("zl", "x", "y", "zh", "core")
SPACE = ("zl", "x")
FILT = ("y", "zh", "core")
BF16 = jnp.bfloat16
F32 = jnp.float32
VMEM = pl.BlockSpec(memory_space=pltpu.VMEM)

GROUPS = 8
CELLS = 512
CHUNKS = 5
ROWS = CHUNKS * 16
OFFSETS = 27
PART = 7


def index_of(zl, x, y, zh, core):
    return (((zl * 4 + x) * 4 + y) * 2 + zh) * 2 + core


def everyone():
    return itertools.product(range(4), range(4), range(4), range(2), range(2))


def pairs_of(move):
    return [(index_of(*place), index_of(*move(*place))) for place in everyone()]


def along(first, step):
    def move(zl, x, y, zh, core):
        if (core == 0) == first:
            return zl, (x - step) % 4, y, zh, core
        return zl, x, (y - step) % 4, zh, core

    return pairs_of(move)


def call(kernel, out_shape, flops=0, byte_count=1 << 20, scratch=(), mib=48):
    single = not isinstance(out_shape, (tuple, list))
    count = 1 if single else len(out_shape)
    return functools.partial(
        pl.pallas_call,
        kernel,
        out_shape=out_shape,
        out_specs=VMEM if single else [VMEM] * count,
        scratch_shapes=list(scratch),
        compiler_params=pltpu.CompilerParams(vmem_limit_bytes=mib << 20),
        cost_estimate=pl.CostEstimate(flops=flops, bytes_accessed=byte_count, transcendentals=0),
    )


def run(kernel, out_shape, *args, **options):
    return call(kernel, out_shape, **options)(in_specs=[VMEM] * len(args))(*args)


def pack_kernel(
    volume_ref, cotangent_ref, filters_ref, packed_ref, send_ref,
    volume, cotangent, filters, slabs_ref, sems,
):
    pairs = ((filters_ref, filters), (volume_ref, volume), (cotangent_ref, cotangent))
    copies = [pltpu.make_async_copy(a, b, sems.at[k]) for k, (a, b) in enumerate(pairs)]
    for copy in copies:
        copy.start()
    copies[0].wait()
    zero = jnp.zeros((16, 16), BF16)
    for outer in range(4):
        offsets = range(8 * outer, 8 * outer + 8)
        block = jnp.concatenate([filters[d] if d < OFFSETS else zero for d in offsets], axis=1)
        for copy in range(8):
            packed_ref[copy, outer] = block
    lane = lax.broadcasted_iota(jnp.int32, (16, 128), 1)
    for part, ref in enumerate((volume, cotangent)):
        copies[1 + part].wait()
        whole = pltpu.roll(ref[...].astype(F32), 64, 1)
        edge = whole[:, :128]
        pieces = [jnp.where(lane < 64, 0.0, edge)]
        pieces += [whole[:, 128 * j : 128 * (j + 1)] for j in range(1, 32)]
        pieces += [jnp.where(lane < 64, edge, 0.0)]
        pieces = [piece.astype(BF16) for piece in pieces]
        for slab in range(GROUPS):
            for chunk in range(CHUNKS):
                row = part * ROWS + chunk * 16
                slabs_ref[slab, row : row + 16, :] = pieces[4 * slab + chunk]
    zh = lax.axis_index("zh")
    for y in range(4):
        send_ref[y] = slabs_ref[2 * y + 1 - zh]


def keep_kernel(volume, cotangent, keep_ref, slabs_ref):
    lane = lax.broadcasted_iota(jnp.int32, (16, 128), 1)
    for part, ref in enumerate((volume, cotangent)):
        whole = pltpu.roll(ref[...].astype(F32), 64, 1)
        edge = whole[:, :128]
        pieces = [jnp.where(lane < 64, 0.0, edge)]
        pieces += [whole[:, 128 * j : 128 * (j + 1)] for j in range(1, 32)]
        pieces += [jnp.where(lane < 64, edge, 0.0)]
        pieces = [piece.astype(BF16) for piece in pieces]
        for slab in range(GROUPS):
            for chunk in range(CHUNKS):
                row = part * ROWS + chunk * 16
                slabs_ref[slab, row : row + 16, :] = pieces[4 * slab + chunk]
    zh = lax.axis_index("zh")
    for y in range(4):
        keep_ref[y] = slabs_ref[2 * y + zh]


def route_kernel(keep_ref, got_ref, *out_refs):
    y, zh = lax.axis_index("y"), lax.axis_index("zh")
    for step, ref in enumerate(out_refs):
        to = lax.rem(y + 4 - step, 4)
        ref[zh] = keep_ref[to]
        ref[1 - zh] = got_ref[to]


def regroup_kernel(packed_ref, out_ref):
    for zl in range(4):
        for outer in range(PART):
            pieces = []
            for d in range(4 * outer, 4 * outer + 4):
                lane = 16 * (d % 8)
                pieces += [packed_ref[2 * zl + zh, d // 8, :, lane : lane + 16] for zh in range(2)]
            out_ref[zl, outer] = jnp.concatenate(pieces, axis=1)


def shifted(pieces):
    whole = jnp.concatenate(pieces, axis=0)
    middle = pltpu.roll(whole.astype(F32), 640 - 64, 1).astype(BF16)
    return whole[:, :CELLS], middle[:, :CELLS], whole[:, 128:]


def block_of(ref, group, first):
    return jnp.concatenate(
        [ref[group, first + 16 * c : first + 16 * (c + 1), :] for c in range(CHUNKS)], axis=1
    )


def turned(value, by):
    return jnp.concatenate([value[:, 128 - by :], value[:, : 128 - by]], axis=1)


def assemble(parts, weights_ref):
    lane = lax.broadcasted_iota(jnp.int32, (PART * 16, 128), 1)
    half, even = lane < 64, lane % 64 < 32

    def turn(pick):
        for zl in range(4):
            for x in range(4):
                row = 16 * (4 * zl + x)
                a, b, c, d = (pick(y, x)[zl].reshape(PART * 16, 128) for y in range(4))
                a, c = jnp.where(half, a, turned(c, 64)), jnp.where(half, turned(a, 64), c)
                b, d = jnp.where(half, b, turned(d, 64)), jnp.where(half, turned(b, 64), d)
                values = (
                    jnp.where(even, a, turned(b, 32)),
                    jnp.where(even, turned(a, 96), b),
                    jnp.where(even, c, turned(d, 32)),
                    jnp.where(even, turned(c, 96), d),
                )
                for outer in range(PART):
                    for k, value in enumerate(values):
                        weights_ref[4 * outer + k, row : row + 16, :] = value[16 * outer : 16 * (outer + 1)]

    @pl.when(lax.axis_index("core") == 0)
    def _():
        turn(lambda y, x: parts[y].at[x])

    @pl.when(lax.axis_index("core") == 1)
    def _():
        turn(lambda y, x: parts[x].at[y])


def combine(before, middle, after):
    place = lax.broadcasted_iota(jnp.int32, middle.shape, 1) % 64
    left = jnp.where(place > 0, pltpu.roll(before, 1, 1), 0.0)
    right = jnp.where(place < 63, pltpu.roll(after, CELLS - 1, 1), 0.0)
    return middle + left + right


def assemble_kernel(part_0, part_1, part_2, part_3, weights_ref):
    assemble((part_0, part_1, part_2, part_3), weights_ref)


def grad_kernel(
    low_ref, own_ref, high_ref, weights_ref, keep_ref, send_ref, stack_ref, result_ref,
):
    for dx, ref in enumerate((high_ref, own_ref, low_ref)):
        above, same, below = shifted([block_of(ref, g, ROWS) for g in range(GROUPS)])
        for dy, value in enumerate((below, same, above)):
            row = (dx * 3 + dy) * 128
            stack_ref[row : row + 128, :] = value
    terms = []
    for dz in range(3):
        left = jnp.concatenate([weights_ref[k * 3 + dz] for k in range(9)], axis=1)
        terms.append(jnp.dot(left, stack_ref[...], preferred_element_type=F32))
    total = combine(terms[2], terms[1], terms[0])
    core, my_x = lax.axis_index("core"), lax.axis_index("x")
    for zl in range(4):
        for step in range(4):
            x = lax.rem(my_x + step, 4)
            row = 16 * (4 * zl + step)
            result_ref[2 * zl + x // 2, lax.rem(x, 2)] = total[row : row + 16]
    keep_ref[...] = result_ref[:, core]
    send_ref[...] = result_ref[:, 1 - core]


def forward_kernel(low_ref, own_ref, high_ref, other_ref, weights_ref, out_ref, volume_ref, stack_ref):
    core, my_x, my_y = (lax.axis_index(name) for name in ("core", "x", "y"))
    for dx, ref in enumerate((low_ref, own_ref, high_ref)):
        for g in range(GROUPS):
            volume_ref[dx, 2 * g + core] = block_of(ref, g, 0)
            volume_ref[dx, 2 * g + 1 - core] = block_of(other_ref.at[dx], g, 0)
        pieces = []
        for zl in range(4):
            for step in range(4):
                x = lax.rem(my_x + step, 4)
                pieces.append(volume_ref[dx, 4 * lax.rem(zl + 4 - my_y, 4) + x])
        for dy, value in enumerate(shifted(pieces)):
            row = (dx * 3 + dy) * 256
            stack_ref[row : row + 256, :] = value
    terms = []
    for dz in range(3):
        left = jnp.concatenate([weights_ref[k * 3 + dz] for k in range(9)], axis=0)
        terms.append(
            lax.dot_general(left, stack_ref[...], (((0,), (0,)), ((), ())), preferred_element_type=F32)
        )
    total = combine(*terms).astype(BF16)
    for step in range(4):
        y = lax.rem(my_y + step, 4)
        for zh in range(2):
            row = 16 * (2 * step + zh)
            out_ref[2 * y + zh] = total[row : row + 16]


def merge_kernel(output_ref, keep_ref, got_ref, out_ref):
    out_ref[:, :16, :] = output_ref[...]
    out_ref[:, 16:, :] = (keep_ref[...] + got_ref[...]).astype(BF16)


def split_kernel(packed_ref, output_ref, grad_ref):
    for g in range(GROUPS):
        output_ref[:, g * CELLS : (g + 1) * CELLS] = packed_ref[g, :16, :]
        grad_ref[:, g * CELLS : (g + 1) * CELLS] = packed_ref[g, 16:, :]


def local(volume, filters, cotangent):
    swap = [(0, 1), (1, 0)]
    half = jax.ShapeDtypeStruct((4, 2 * ROWS, 128), BF16)
    packed, send = call(
        pack_kernel,
        [jax.ShapeDtypeStruct((8, 4, 16, 128), BF16), half],
        scratch=[
            pltpu.VMEM((16, 4096), BF16),
            pltpu.VMEM((16, 4096), BF16),
            pltpu.VMEM((OFFSETS, 16, 16), BF16),
            pltpu.VMEM((GROUPS, 2 * ROWS, 128), BF16),
            pltpu.SemaphoreType.DMA((3,)),
        ],
        mib=60,
    )(in_specs=[pl.BlockSpec(memory_space=pl.ANY)] * 3)(
        volume.reshape(16, 4096),
        cotangent.reshape(16, 4096),
        filters.reshape(OFFSETS, 16, 16),
    )
    got = lax.ppermute(send, "zh", swap)
    keep = run(
        keep_kernel,
        half,
        volume.reshape(16, 4096),
        cotangent.reshape(16, 4096),
        scratch=[pltpu.VMEM((GROUPS, 2 * ROWS, 128), BF16)],
    )
    packed = lax.all_to_all(packed, ("zl", "zh"), 0, 0)
    routed = run(route_kernel, [jax.ShapeDtypeStruct((2, 2 * ROWS, 128), BF16)] * 4, keep, got)
    own = [routed[0]]
    for step in (1, 2, 3):
        own.append(lax.ppermute(routed[step], "y", [(i, (i - step) % 4) for i in range(4)]))
    own = jnp.stack(own).reshape(GROUPS, 2 * ROWS, 128)
    unit = run(regroup_kernel, jax.ShapeDtypeStruct((4, PART, 16, 128), BF16), packed)

    def gather(block, pairs):
        return [block] + [lax.ppermute(block, AXES, pairs(step)) for step in (1, 2, 3)]

    unit = jnp.stack(gather(unit, functools.partial(along, True)))
    own, _ = lax.optimization_barrier((own, unit))
    parts = gather(unit, functools.partial(along, False))
    up = [(i, i + 1) for i in range(15)]
    down = [(b, a) for a, b in up]
    low = lax.ppermute(own, SPACE, up)
    high = lax.ppermute(own, SPACE, down)
    flops = 2 * 27 * 256 * 128 * CELLS
    piece = jax.ShapeDtypeStruct((GROUPS, 16, CELLS), F32)
    weights = run(
        assemble_kernel,
        jax.ShapeDtypeStruct((4 * PART, 256, 128), BF16),
        *parts,
        byte_count=64 << 20,
    )
    low, high, weights = lax.optimization_barrier((low, high, weights))
    other = lax.ppermute(jnp.stack([low[:, :ROWS], own[:, :ROWS], high[:, :ROWS]]), "core", swap)
    keep, send = run(
        grad_kernel,
        [piece, piece],
        low,
        own,
        high,
        weights,
        flops=flops,
        byte_count=4 << 20,
        scratch=[pltpu.VMEM((9 * 128, CELLS), BF16), pltpu.VMEM((GROUPS, 2, 16, CELLS), F32)],
    )
    got = lax.ppermute(send, "core", swap)
    output = run(
        forward_kernel,
        jax.ShapeDtypeStruct((GROUPS, 16, CELLS), BF16),
        low,
        own,
        high,
        other,
        weights,
        flops=flops,
        byte_count=4 << 20,
        scratch=[
            pltpu.VMEM((3, 16, 16, CHUNKS * 128), BF16),
            pltpu.VMEM((9 * 256, CELLS), BF16),
        ],
    )
    merged = run(merge_kernel, jax.ShapeDtypeStruct((GROUPS, 32, CELLS), BF16), output, keep, got)
    merged = lax.all_to_all(merged, ("y", "zh"), 0, 0)
    plane = jax.ShapeDtypeStruct((16, 4096), BF16)
    output, grad = run(split_kernel, [plane, plane], merged)
    return output.reshape(16, 1, 4096), grad.reshape(16, 1, 4096)


def solution(mesh):
    split = Mesh(mesh.devices.reshape(4, 4, 4, 2, 2), AXES)
    act = P(FILT, SPACE, None)
    return jax.shard_map(
        local,
        mesh=split,
        in_specs=(act, P(None, None, None, SPACE, FILT), act),
        out_specs=(act, act),
        check_vma=False,
    )
```

```python
import functools
import itertools

import jax
import jax.numpy as jnp
from jax import lax
from jax.experimental import pallas as pl
from jax.experimental.pallas import tpu as pltpu
from jax.sharding import Mesh
from jax.sharding import PartitionSpec as P

AXES = ("zl", "x", "y", "zh", "core")
SPACE = ("zl", "x")
FILT = ("y", "zh", "core")
BF16 = jnp.bfloat16
F32 = jnp.float32
VMEM = pl.BlockSpec(memory_space=pltpu.VMEM)

GROUPS = 8
CELLS = 512
CHUNKS = 5
ROWS = CHUNKS * 16
OFFSETS = 27
PART = 7


def index_of(zl, x, y, zh, core):
    return (((zl * 4 + x) * 4 + y) * 2 + zh) * 2 + core


def everyone():
    return itertools.product(range(4), range(4), range(4), range(2), range(2))


def pairs_of(move):
    return [(index_of(*place), index_of(*move(*place))) for place in everyone()]


def along(first, step):
    def move(zl, x, y, zh, core):
        if (core == 0) == first:
            return zl, (x - step) % 4, y, zh, core
        return zl, x, (y - step) % 4, zh, core

    return pairs_of(move)


def call(kernel, out_shape, flops=0, byte_count=1 << 20, scratch=(), mib=48):
    single = not isinstance(out_shape, (tuple, list))
    count = 1 if single else len(out_shape)
    return functools.partial(
        pl.pallas_call,
        kernel,
        out_shape=out_shape,
        out_specs=VMEM if single else [VMEM] * count,
        scratch_shapes=list(scratch),
        compiler_params=pltpu.CompilerParams(vmem_limit_bytes=mib << 20),
        cost_estimate=pl.CostEstimate(flops=flops, bytes_accessed=byte_count, transcendentals=0),
    )


def run(kernel, out_shape, *args, **options):
    return call(kernel, out_shape, **options)(in_specs=[VMEM] * len(args))(*args)


def pack_kernel(
    volume_ref, cotangent_ref, filters_ref, packed_ref, send_ref,
    volume, cotangent, filters, slabs_ref, sems,
):
    pairs = ((filters_ref, filters), (volume_ref, volume), (cotangent_ref, cotangent))
    copies = [pltpu.make_async_copy(a, b, sems.at[k]) for k, (a, b) in enumerate(pairs)]
    for copy in copies:
        copy.start()
    copies[0].wait()
    zero = jnp.zeros((16, 16), BF16)
    for outer in range(4):
        offsets = range(8 * outer, 8 * outer + 8)
        block = jnp.concatenate([filters[d] if d < OFFSETS else zero for d in offsets], axis=1)
        for copy in range(8):
            packed_ref[copy, outer] = block
    lane = lax.broadcasted_iota(jnp.int32, (16, 128), 1)
    for part, ref in enumerate((volume, cotangent)):
        copies[1 + part].wait()
        whole = pltpu.roll(ref[...].astype(F32), 64, 1)
        edge = whole[:, :128]
        pieces = [jnp.where(lane < 64, 0.0, edge)]
        pieces += [whole[:, 128 * j : 128 * (j + 1)] for j in range(1, 32)]
        pieces += [jnp.where(lane < 64, edge, 0.0)]
        pieces = [piece.astype(BF16) for piece in pieces]
        for slab in range(GROUPS):
            for chunk in range(CHUNKS):
                row = part * ROWS + chunk * 16
                slabs_ref[slab, row : row + 16, :] = pieces[4 * slab + chunk]
    zh = lax.axis_index("zh")
    for y in range(4):
        send_ref[y] = slabs_ref[2 * y + 1 - zh]


def keep_kernel(volume, cotangent, keep_ref, slabs_ref):
    lane = lax.broadcasted_iota(jnp.int32, (16, 128), 1)
    for part, ref in enumerate((volume, cotangent)):
        whole = pltpu.roll(ref[...].astype(F32), 64, 1)
        edge = whole[:, :128]
        pieces = [jnp.where(lane < 64, 0.0, edge)]
        pieces += [whole[:, 128 * j : 128 * (j + 1)] for j in range(1, 32)]
        pieces += [jnp.where(lane < 64, edge, 0.0)]
        pieces = [piece.astype(BF16) for piece in pieces]
        for slab in range(GROUPS):
            for chunk in range(CHUNKS):
                row = part * ROWS + chunk * 16
                slabs_ref[slab, row : row + 16, :] = pieces[4 * slab + chunk]
    zh = lax.axis_index("zh")
    for y in range(4):
        keep_ref[y] = slabs_ref[2 * y + zh]


def route_kernel(keep_ref, got_ref, *out_refs):
    y, zh = lax.axis_index("y"), lax.axis_index("zh")
    for step, ref in enumerate(out_refs):
        to = lax.rem(y + 4 - step, 4)
        ref[zh] = keep_ref[to]
        ref[1 - zh] = got_ref[to]


def regroup_kernel(packed_ref, out_ref):
    for zl in range(4):
        for outer in range(PART):
            pieces = []
            for d in range(4 * outer, 4 * outer + 4):
                lane = 16 * (d % 8)
                pieces += [packed_ref[2 * zl + zh, d // 8, :, lane : lane + 16] for zh in range(2)]
            out_ref[zl, outer] = jnp.concatenate(pieces, axis=1)


def shifted(pieces):
    whole = jnp.concatenate(pieces, axis=0)
    middle = pltpu.roll(whole.astype(F32), 640 - 64, 1).astype(BF16)
    return whole[:, :CELLS], middle[:, :CELLS], whole[:, 128:]


def block_of(ref, group, first):
    return jnp.concatenate(
        [ref[group, first + 16 * c : first + 16 * (c + 1), :] for c in range(CHUNKS)], axis=1
    )


def turned(value, by):
    return jnp.concatenate([value[:, 128 - by :], value[:, : 128 - by]], axis=1)


def assemble(parts, weights_ref):
    lane = lax.broadcasted_iota(jnp.int32, (PART * 16, 128), 1)
    half, even = lane < 64, lane % 64 < 32

    def turn(pick):
        for zl in range(4):
            for x in range(4):
                row = 16 * (4 * zl + x)
                a, b, c, d = (pick(y, x)[zl].reshape(PART * 16, 128) for y in range(4))
                a, c = jnp.where(half, a, turned(c, 64)), jnp.where(half, turned(a, 64), c)
                b, d = jnp.where(half, b, turned(d, 64)), jnp.where(half, turned(b, 64), d)
                values = (
                    jnp.where(even, a, turned(b, 32)),
                    jnp.where(even, turned(a, 96), b),
                    jnp.where(even, c, turned(d, 32)),
                    jnp.where(even, turned(c, 96), d),
                )
                for outer in range(PART):
                    for k, value in enumerate(values):
                        weights_ref[4 * outer + k, row : row + 16, :] = value[16 * outer : 16 * (outer + 1)]

    @pl.when(lax.axis_index("core") == 0)
    def _():
        turn(lambda y, x: parts[y].at[x])

    @pl.when(lax.axis_index("core") == 1)
    def _():
        turn(lambda y, x: parts[x].at[y])


def combine(before, middle, after):
    place = lax.broadcasted_iota(jnp.int32, middle.shape, 1) % 64
    left = jnp.where(place > 0, pltpu.roll(before, 1, 1), 0.0)
    right = jnp.where(place < 63, pltpu.roll(after, CELLS - 1, 1), 0.0)
    return middle + left + right


def assemble_kernel(part_0, part_1, part_2, part_3, weights_ref):
    assemble((part_0, part_1, part_2, part_3), weights_ref)


def grad_kernel(
    low_ref, own_ref, high_ref, weights_ref, keep_ref, send_ref, stack_ref, result_ref,
):
    for dx, ref in enumerate((high_ref, own_ref, low_ref)):
        above, same, below = shifted([block_of(ref, g, ROWS) for g in range(GROUPS)])
        for dy, value in enumerate((below, same, above)):
            row = (dx * 3 + dy) * 128
            stack_ref[row : row + 128, :] = value
    terms = []
    for dz in range(3):
        left = jnp.concatenate([weights_ref[k * 3 + dz] for k in range(9)], axis=1)
        terms.append(jnp.dot(left, stack_ref[...], preferred_element_type=F32))
    total = combine(terms[2], terms[1], terms[0])
    core, my_x = lax.axis_index("core"), lax.axis_index("x")
    for zl in range(4):
        for step in range(4):
            x = lax.rem(my_x + step, 4)
            row = 16 * (4 * zl + step)
            result_ref[2 * zl + x // 2, lax.rem(x, 2)] = total[row : row + 16]
    keep_ref[...] = result_ref[:, core]
    send_ref[...] = result_ref[:, 1 - core]


def forward_kernel(low_ref, own_ref, high_ref, other_ref, weights_ref, out_ref, volume_ref, stack_ref):
    core, my_x, my_y = (lax.axis_index(name) for name in ("core", "x", "y"))
    for dx, ref in enumerate((low_ref, own_ref, high_ref)):
        for g in range(GROUPS):
            volume_ref[dx, 2 * g + core] = block_of(ref, g, 0)
            volume_ref[dx, 2 * g + 1 - core] = block_of(other_ref.at[dx], g, 0)
        pieces = []
        for zl in range(4):
            for step in range(4):
                x = lax.rem(my_x + step, 4)
                pieces.append(volume_ref[dx, 4 * lax.rem(zl + 4 - my_y, 4) + x])
        for dy, value in enumerate(shifted(pieces)):
            row = (dx * 3 + dy) * 256
            stack_ref[row : row + 256, :] = value
    terms = []
    for dz in range(3):
        left = jnp.concatenate([weights_ref[k * 3 + dz] for k in range(9)], axis=0)
        terms.append(
            lax.dot_general(left, stack_ref[...], (((0,), (0,)), ((), ())), preferred_element_type=F32)
        )
    total = combine(*terms).astype(BF16)
    for step in range(4):
        y = lax.rem(my_y + step, 4)
        for zh in range(2):
            row = 16 * (2 * step + zh)
            out_ref[2 * y + zh] = total[row : row + 16]


def merge_kernel(output_ref, keep_ref, got_ref, out_ref):
    out_ref[:, :16, :] = output_ref[...]
    out_ref[:, 16:, :] = (keep_ref[...] + got_ref[...]).astype(BF16)


def split_kernel(packed_ref, output_ref, grad_ref):
    for g in range(GROUPS):
        output_ref[:, g * CELLS : (g + 1) * CELLS] = packed_ref[g, :16, :]
        grad_ref[:, g * CELLS : (g + 1) * CELLS] = packed_ref[g, 16:, :]


def local(volume, filters, cotangent):
    swap = [(0, 1), (1, 0)]
    half = jax.ShapeDtypeStruct((4, 2 * ROWS, 128), BF16)
    packed, send = call(
        pack_kernel,
        [jax.ShapeDtypeStruct((8, 4, 16, 128), BF16), half],
        scratch=[
            pltpu.VMEM((16, 4096), BF16),
            pltpu.VMEM((16, 4096), BF16),
            pltpu.VMEM((OFFSETS, 16, 16), BF16),
            pltpu.VMEM((GROUPS, 2 * ROWS, 128), BF16),
            pltpu.SemaphoreType.DMA((3,)),
        ],
        mib=60,
    )(in_specs=[pl.BlockSpec(memory_space=pl.ANY)] * 3)(
        volume.reshape(16, 4096),
        cotangent.reshape(16, 4096),
        filters.reshape(OFFSETS, 16, 16),
    )
    got = lax.ppermute(send, "zh", swap)
    keep = run(
        keep_kernel,
        half,
        volume.reshape(16, 4096),
        cotangent.reshape(16, 4096),
        scratch=[pltpu.VMEM((GROUPS, 2 * ROWS, 128), BF16)],
    )
    packed = lax.all_to_all(packed, ("zl", "zh"), 0, 0)
    routed = run(route_kernel, [jax.ShapeDtypeStruct((2, 2 * ROWS, 128), BF16)] * 4, keep, got)
    own = [routed[0]]
    for step in (1, 2, 3):
        own.append(lax.ppermute(routed[step], "y", [(i, (i - step) % 4) for i in range(4)]))
    own = jnp.stack(own).reshape(GROUPS, 2 * ROWS, 128)
    unit = run(regroup_kernel, jax.ShapeDtypeStruct((4, PART, 16, 128), BF16), packed)

    def gather(block, pairs):
        got = {step: lax.ppermute(block, AXES, pairs(step)) for step in (2, 1, 3)}
        return [block, got[1], got[2], got[3]]

    unit = jnp.stack(gather(unit, functools.partial(along, True)))
    own, _ = lax.optimization_barrier((own, unit))
    parts = gather(unit, functools.partial(along, False))
    up = [(i, i + 1) for i in range(15)]
    down = [(b, a) for a, b in up]
    low = lax.ppermute(own, SPACE, up)
    high = lax.ppermute(own, SPACE, down)
    flops = 2 * 27 * 256 * 128 * CELLS
    piece = jax.ShapeDtypeStruct((GROUPS, 16, CELLS), F32)
    weights = run(
        assemble_kernel,
        jax.ShapeDtypeStruct((4 * PART, 256, 128), BF16),
        *parts,
        byte_count=64 << 20,
    )
    low, high, weights = lax.optimization_barrier((low, high, weights))
    other = lax.ppermute(jnp.stack([low[:, :ROWS], own[:, :ROWS], high[:, :ROWS]]), "core", swap)
    keep, send = run(
        grad_kernel,
        [piece, piece],
        low,
        own,
        high,
        weights,
        flops=flops,
        byte_count=4 << 20,
        scratch=[pltpu.VMEM((9 * 128, CELLS), BF16), pltpu.VMEM((GROUPS, 2, 16, CELLS), F32)],
    )
    got = lax.ppermute(send, "core", swap)
    output = run(
        forward_kernel,
        jax.ShapeDtypeStruct((GROUPS, 16, CELLS), BF16),
        low,
        own,
        high,
        other,
        weights,
        flops=flops,
        byte_count=4 << 20,
        scratch=[
            pltpu.VMEM((3, 16, 16, CHUNKS * 128), BF16),
            pltpu.VMEM((9 * 256, CELLS), BF16),
        ],
    )
    merged = run(merge_kernel, jax.ShapeDtypeStruct((GROUPS, 32, CELLS), BF16), output, keep, got)
    merged = lax.all_to_all(merged, ("y", "zh"), 0, 0)
    plane = jax.ShapeDtypeStruct((16, 4096), BF16)
    output, grad = run(split_kernel, [plane, plane], merged)
    return output.reshape(16, 1, 4096), grad.reshape(16, 1, 4096)


def solution(mesh):
    split = Mesh(mesh.devices.reshape(4, 4, 4, 2, 2), AXES)
    act = P(FILT, SPACE, None)
    return jax.shard_map(
        local,
        mesh=split,
        in_specs=(act, P(None, None, None, SPACE, FILT), act),
        out_specs=(act, act),
        check_vma=False,
    )
```
